32 devices in a mesh: tower: 4 (over y, core), dev: 8 (over z, x).
Axes of the slice: x: 2, y: 2, z: 4, core: 2. Of those that a mesh axis runs over, the one named last changes fastest.
Arguments:
- bag_ids: int32 [4, 1024, 32, 4], P('tower', None, 'dev'), may hold values from 0 to 1023
- bag_lengths: int32 [4, 1024, 32], P('tower', None, 'dev'), may hold values from 1 to 4
- tables: bfloat16 [4, 32, 1024, 128], P('tower', 'dev'), may hold values from -3 to 3
- cross_down: bfloat16 [4, 1, 4096, 512], P('tower'), may hold values from -0.09375 to 0.09375
- cross_up: bfloat16 [4, 1, 512, 4096], P('tower'), may hold values from -0.25 to 0.25
- cross_bias: float32 [4, 1, 4096], P('tower'), may hold values from -4 to 4
- proj_weight: bfloat16 [4, 4096, 512], P('tower'), may hold values from -0.09375 to 0.09375
- proj_bias: float32 [4, 512], P('tower'), may hold values from -3 to 3
Outputs:
- interactions: float32 [1024, 6], P(('tower', 'dev'))
The draws below stay inside these ranges and needn't reach their ends.
Inputs may be any that keep to these rules, and one draw needn't show every extreme that they name: `bag_ids`: where table rows travel between devices, each is sent as a whole 32-bit integer, one to a slot; a program may not pack several table rows into one word. `bag_lengths`: where bag lengths travel between devices, a program may pack several of them into one word.
All inputs are finite; a program needn't handle non-finite values.
Results may differ from the reference program's by a relative error of at most 0.0071.
Values may be sent and summed in bfloat16 or wider, within the bound.
No kernel may reach another device: no remote copies, remote signals or barrier semaphores. Data moves between devices by JAX's collectives and lax.ppermute only.
A program may use at most 128 MiB of HBM per device.

```python
import jax
import jax.numpy as jnp
import numpy as np
from jax import lax

EMB = 128
FEATS = 32
D = 4096
RANK = 512
OUT = 512
LAYERS = 1
POOL = 4
TROWS = 1024
TOWERS = 4
SAMPLES = 1024


def with_ends(entries, own_key, least, high):
    index_at = [jax.random.randint(jax.random.fold_in(own_key, axis), (), 0, length) for axis, length in enumerate(entries.shape)]
    longest = entries.shape.index(max(entries.shape))
    beside = index_at[:longest] + [(index_at[longest] + 1) % entries.shape[longest]] + index_at[longest + 1:]
    return entries.at[tuple(index_at)].set(least).at[tuple(beside)].set(high)


def steps_of(own_key, dims, shards, smallest, high):
    def one(position, blocks):
        heights = jax.random.uniform(jax.random.fold_in(jax.random.fold_in(own_key, 6), position), (blocks,), jnp.float32, smallest / len(shards), high / len(shards))
        return jnp.repeat(jnp.exp(heights), dims[position] // blocks).reshape((-1,) + (1,) * (len(dims) - position - 1))

    factor_of = one(*shards[0])
    for cut in shards[1:]:
        factor_of = factor_of * one(*cut)
    return factor_of


def noise(stream_key, shape, scale, reach, split=(), kind=jnp.bfloat16):
    entries = scale * jax.random.normal(stream_key, shape, jnp.float32)
    if split:
        entries = entries * steps_of(stream_key, shape, split, -0.22, 0.18)
    return jnp.clip(entries, -reach, reach).astype(kind)


def setup_inputs(seed: int = 0) -> dict:
    streams_of = jax.random.split(jax.random.key(seed), 9)
    return {
        "bag_ids": with_ends(jax.random.randint(streams_of[0], (TOWERS, SAMPLES, FEATS, POOL), 0, TROWS), jax.random.fold_in(streams_of[0], 1), 0, TROWS - 1).astype(jnp.int32),
        "bag_lengths": with_ends(jax.random.randint(streams_of[1], (TOWERS, SAMPLES, FEATS), 1, POOL + 1), jax.random.fold_in(streams_of[1], 1), 1, POOL).astype(jnp.int32),
        "tables": noise(streams_of[2], (TOWERS, FEATS, TROWS, EMB), 0.5, 3.0, ((0, 4), (1, 8))),
        "cross_down": noise(streams_of[3], (TOWERS, LAYERS, D, RANK), D ** -0.5, 0.09375, ((0, 4),)),
        "cross_up": noise(streams_of[4], (TOWERS, LAYERS, RANK, D), RANK ** -0.5, 0.25, ((0, 4),)),
        "cross_bias": noise(streams_of[5], (TOWERS, LAYERS, D), 1.0, 4.0, ((0, 4),), jnp.float32),
        "proj_weight": noise(streams_of[6], (TOWERS, D, OUT), D ** -0.5, 0.09375, ((0, 4),)),
        "proj_bias": noise(streams_of[7], (TOWERS, OUT), 0.5, 3.0, ((0, 4),), jnp.float32),
    }


def pool_rows(tables_one, ids_one, lengths_one):
    total = jnp.zeros(ids_one.shape[:2] + (tables_one.shape[2],), jnp.float32)
    for slot in range(ids_one.shape[2]):
        rows = jax.vmap(lambda table, index: jnp.take(table, index, axis=0), in_axes=(0, 1), out_axes=1)(tables_one, ids_one[:, :, slot])
        live = (slot < lengths_one).astype(jnp.float32)[:, :, None]
        total = total + rows.astype(jnp.float32) * live
    return total.astype(jnp.bfloat16)

def tower_forward(base, down, up, bias, proj, proj_b):
    base_f = base.astype(jnp.float32)
    cross = base
    for layer in range(down.shape[0]):
        low = jnp.dot(cross, down[layer], preferred_element_type=jnp.float32).astype(jnp.bfloat16)
        high = jnp.dot(low, up[layer], preferred_element_type=jnp.float32) + bias[layer]
        cross = (base_f * high + cross.astype(jnp.float32)).astype(jnp.bfloat16)
    return (jnp.dot(cross, proj, preferred_element_type=jnp.float32) + proj_b).astype(jnp.bfloat16)

def one_tower(packed):
    ids_one, lengths_one, tables_one, down, up, bias, proj, proj_b = packed
    pooled = pool_rows(tables_one, ids_one, lengths_one)
    base = pooled.reshape(pooled.shape[0], -1)
    return tower_forward(base, down, up, bias, proj, proj_b)

def reference(bag_ids, bag_lengths, tables, cross_down, cross_up, cross_bias, proj_weight, proj_bias):
    outputs = lax.map(one_tower, (bag_ids, bag_lengths, tables, cross_down, cross_up, cross_bias, proj_weight, proj_bias))
    wide = outputs.astype(jnp.float32)
    gram = jnp.einsum('isk,jsk->sij', wide, wide) / jnp.sqrt(jnp.float32(OUT))
    upper, lower = np.triu_indices(TOWERS, 1)
    return gram[:, upper, lower]
```

```python
import functools

import jax
import jax.numpy as jnp
import numpy as np
from jax import lax
from jax.experimental import pallas as pl
from jax.experimental.pallas import tpu as pltpu
from jax.sharding import PartitionSpec as P

LANES = 128
MIB = 1 << 20


def pool_kernel(block, feats, slots, me_ref, ids_ref, len_ref, tab_ref, after_ref, *rest):
    outs, scratch = rest[:-1], rest[-1]
    per = len(outs)
    rows = tab_ref.shape[1]
    lens = len_ref[...]
    stack = []
    for f in range(feats):
        ids = ids_ref[f]
        slot = lax.broadcasted_iota(jnp.int32, ids.shape, 0)
        ids = jnp.where(slot < lens[f : f + 1], ids, -1)
        times = jnp.zeros(ids.shape, jnp.float32)
        for p in range(slots):
            times += jnp.where(ids == ids[p : p + 1], 1.0, 0.0)
        stack += [ids.astype(jnp.float32), times]
    stack = jnp.concatenate(stack, axis=0)
    pad = -stack.shape[0] % LANES
    if pad:
        stack = jnp.concatenate([stack, jnp.zeros((pad, LANES), jnp.float32)], axis=0)
    cols = stack.T
    place = lax.broadcasted_iota(jnp.int16, (LANES, rows), 1)
    for f in range(feats):
        counts = jnp.zeros((LANES, rows), jnp.bfloat16)
        for p in range(slots):
            c = 2 * slots * f + p
            own = cols[:, c : c + 1].astype(jnp.int32).astype(jnp.int16)
            times = cols[:, c + slots : c + slots + 1].astype(jnp.bfloat16)
            counts = jnp.where(place == own, times, counts)
        total = jnp.dot(counts, tab_ref[f], preferred_element_type=jnp.float32)
        scratch[:, f * LANES : (f + 1) * LANES] = total.astype(jnp.bfloat16)
    low = lax.rem(me_ref[0], per)
    for k in range(per):
        start = pl.multiple_of((low ^ k) * block, block)
        outs[k][...] = scratch[pl.ds(start, block), :]


def pool_group(me, ids, lens, tables, after, group, towers, members, block):
    feats, slots, samples = ids.shape
    width = tables.shape[2]
    per = LANES // block
    groups = members // per

    def tile(t, me_ref):
        return t * groups + (me_ref[0] // per ^ group)

    shape = jax.ShapeDtypeStruct((towers * block, feats * width), jnp.bfloat16)
    return pl.pallas_call(
        functools.partial(pool_kernel, block, feats, slots),
        grid_spec=pltpu.PrefetchScalarGridSpec(
            num_scalar_prefetch=1,
            grid=(towers,),
            in_specs=[
                pl.BlockSpec((feats, slots, LANES), lambda t, m: (0, 0, tile(t, m))),
                pl.BlockSpec((feats, LANES), lambda t, m: (0, tile(t, m))),
                pl.BlockSpec(tables.shape, lambda t, m: (0, 0, 0)),
                pl.BlockSpec(memory_space=pl.ANY),
            ],
            out_specs=[pl.BlockSpec((block, feats * width), lambda t, m: (t, 0))] * per,
            scratch_shapes=[pltpu.VMEM((LANES, feats * width), jnp.bfloat16)],
        ),
        out_shape=[shape] * per,
        compiler_params=pltpu.CompilerParams(vmem_limit_bytes=24 * MIB),
        cost_estimate=pl.CostEstimate(
            flops=2 * towers * LANES * feats * tables.shape[1] * width * 8,
            bytes_accessed=tables.size * 2,
            transcendentals=0,
        ),
        name="pool_group",
    )(me, ids, lens, tables, after)


def low_kernel(order, me_ref, down_ref, *rest):
    chunks, out_ref = rest[:-1], rest[-1]
    depth = chunks[0].shape[1]
    total = None
    for k, chunk in zip(order, chunks, strict=True):
        start = pl.multiple_of((me_ref[0] ^ k) * depth, depth)
        part = jnp.dot(
            chunk[...], down_ref[pl.ds(start, depth), :], preferred_element_type=jnp.float32
        )
        total = part if total is None else total + part
    out_ref[...] = total


def low_part(me, down, chunks, order):
    rows = chunks[0].shape[0]
    return pl.pallas_call(
        functools.partial(low_kernel, order),
        in_specs=[pl.BlockSpec(memory_space=pltpu.SMEM)]
        + [pl.BlockSpec(memory_space=pltpu.VMEM)] * (1 + len(chunks)),
        out_specs=pl.BlockSpec(memory_space=pltpu.VMEM),
        out_shape=jax.ShapeDtypeStruct((rows, down.shape[1]), jnp.float32),
        compiler_params=pltpu.CompilerParams(vmem_limit_bytes=24 * MIB),
        cost_estimate=pl.CostEstimate(
            flops=2 * rows * chunks[0].shape[1] * len(chunks) * down.shape[1],
            bytes_accessed=down.size * 2,
            transcendentals=0,
        ),
        name="low_part",
    )(me, down, *chunks)


def tower_kernel(near, far, me_ref, low_ref, down_ref, up_ref, bias_ref, proj_ref, pb_ref, *rest):
    chunks, outs, scratch = rest[: len(near) + len(far)], rest[len(near) + len(far) : -1], rest[-1]
    depth = chunks[0].shape[1]
    block = outs[0].shape[0]
    order = near + far

    def place(k):
        return pl.ds(pl.multiple_of((me_ref[0] ^ k) * depth, depth), depth)

    low = low_ref[...]
    for k, chunk in list(zip(order, chunks, strict=True))[len(near) :]:
        low += jnp.dot(chunk[...], down_ref[place(k), :], preferred_element_type=jnp.float32)
    low = low.astype(jnp.bfloat16)
    total = pb_ref[...]
    for k, chunk in zip(order, chunks, strict=True):
        high = jnp.dot(low, up_ref[:, place(k)], preferred_element_type=jnp.float32)
        high = high + bias_ref[:, place(k)]
        base = chunk[...].astype(jnp.float32)
        cross = (base * high + base).astype(jnp.bfloat16)
        total = total + jnp.dot(cross, proj_ref[place(k), :], preferred_element_type=jnp.float32)
    scratch[...] = total.astype(jnp.bfloat16)
    for k, out in enumerate(outs):
        out[...] = scratch[pl.ds(pl.multiple_of((me_ref[1] ^ k) * block, block), block), :]


def tower_out(me, low, down, up, bias, proj, pb, chunks, near, far, towers):
    rows = chunks[0].shape[0]
    shape = jax.ShapeDtypeStruct((rows // towers, proj.shape[1]), jnp.bfloat16)
    return pl.pallas_call(
        functools.partial(tower_kernel, near, far),
        in_specs=[pl.BlockSpec(memory_space=pltpu.SMEM)]
        + [pl.BlockSpec(memory_space=pltpu.VMEM)] * (6 + len(chunks)),
        out_specs=[pl.BlockSpec(memory_space=pltpu.VMEM)] * towers,
        out_shape=[shape] * towers,
        scratch_shapes=[pltpu.VMEM((rows, proj.shape[1]), jnp.bfloat16)],
        compiler_params=pltpu.CompilerParams(vmem_limit_bytes=32 * MIB),
        cost_estimate=pl.CostEstimate(
            flops=4 * rows * proj.size, bytes_accessed=proj.size * 4, transcendentals=0
        ),
        name="tower_out",
    )(me, low, down, up, bias, proj, pb, *chunks)


def gram_kernel(me_ref, *rest):
    chunks, out_ref, rows_ref = rest[:-2], rest[-2], rest[-1]
    towers, (block, width) = len(chunks), chunks[0].shape
    for k, chunk in enumerate(chunks):
        rows_ref[me_ref[1] ^ k] = chunk[...]
    rows = rows_ref[...].reshape(towers * block, width)
    gram = lax.dot_general(
        rows, rows, (((1,), (1,)), ((), ())), preferred_element_type=jnp.float32
    ) * (1.0 / np.sqrt(np.float32(width)))
    n = towers * block
    at = lax.broadcasted_iota(jnp.int32, (block, n), 0)
    to = lax.broadcasted_iota(jnp.int32, (block, n), 1)
    own = at == lax.rem(to, block)
    place = 0
    for i in range(towers):
        picked = jnp.where(own, gram[i * block : (i + 1) * block], 0.0)
        line = jnp.sum(picked, axis=0, keepdims=True)
        for j in range(i + 1, towers):
            out_ref[place : place + 1, :] = line[:, j * block : (j + 1) * block]
            place += 1


def gram_pairs(me, chunks):
    towers, (block, width) = len(chunks), chunks[0].shape
    pairs = towers * (towers - 1) // 2
    return pl.pallas_call(
        gram_kernel,
        in_specs=[pl.BlockSpec(memory_space=pltpu.SMEM)]
        + [pl.BlockSpec(memory_space=pltpu.VMEM)] * towers,
        out_specs=pl.BlockSpec(memory_space=pltpu.VMEM),
        out_shape=jax.ShapeDtypeStruct((pairs, block), jnp.float32),
        scratch_shapes=[pltpu.VMEM((towers, block, width), jnp.bfloat16)],
        compiler_params=pltpu.CompilerParams(vmem_limit_bytes=16 * MIB),
        name="gram_pairs",
    )(me, *chunks)


def swap(x, axis, k):
    size = lax.axis_size(axis)
    return lax.ppermute(x, axis, [(i, i ^ k) for i in range(size)])


def local(bag_ids, bag_lengths, tables, cross_down, cross_up, cross_bias, proj_weight, proj_bias):
    towers = lax.axis_size("tower")
    members = lax.axis_size("dev")
    samples = bag_ids.shape[1]
    block = samples // (towers * members)
    per = LANES // block
    groups = members // per
    me = jnp.stack([lax.axis_index("dev"), lax.axis_index("tower")])
    ids = bag_ids[0].transpose(1, 2, 0)
    lens = bag_lengths[0].transpose(1, 0)
    after = lens
    pooled = {}
    for g in range(groups - 1, -1, -1):
        parts = pool_group(me, ids, lens, tables[0], after, g, towers, members, block)
        after = parts[0]
        for k, part in enumerate(parts):
            pooled[g * per + k] = part
    near = tuple(range(per))
    far = tuple(range(per, members))
    arrived = {0: pooled[0]}
    for k in range(members - 1, 0, -1):
        arrived[k] = swap(pooled[k], "dev", k)
    down, up, bias = cross_down[0, 0], cross_up[0, 0], cross_bias[0]
    low = low_part(me, down, [arrived[k] for k in near], near)
    outs = tower_out(
        me, low, down, up, bias, proj_weight[0], proj_bias,
        [arrived[k] for k in near + far], near, far, towers,
    )
    met = {0: outs[0]}
    for k in range(towers - 1, 0, -1):
        met[k] = swap(outs[k], "tower", k)
    return gram_pairs(me, [met[k] for k in range(towers)]).T


def solution(mesh):
    placed = (
        P("tower", None, "dev", None),
        P("tower", None, "dev"),
        P("tower", "dev", None, None),
        P("tower", None, None, None),
        P("tower", None, None, None),
        P("tower", None, None),
        P("tower", None, None),
        P("tower", None),
    )
    return jax.shard_map(
        local, mesh=mesh, in_specs=placed, out_specs=P(("tower", "dev"), None), check_vma=False
    )
```

```python
import functools

import jax
import jax.numpy as jnp
import numpy as np
from jax import lax
from jax.experimental import pallas as pl
from jax.experimental.pallas import tpu as pltpu
from jax.sharding import PartitionSpec as P

LANES = 128
MIB = 1 << 20
BATCH = 512
ANY = pl.BlockSpec(memory_space=pl.ANY)
VMEM = pl.BlockSpec(memory_space=pltpu.VMEM)


def bag_tiles(group, block, towers, ids_ref, len_ref):
    feats, slots, samples = ids_ref.shape
    groups = samples // (towers * LANES)
    tiles = []
    for t in range(towers):
        at = pl.ds(pl.multiple_of((t * groups + group) * LANES, LANES), LANES)
        lens = len_ref[:, at]
        rows = []
        for f in range(feats):
            ids = ids_ref[f, :, at]
            slot = lax.broadcasted_iota(jnp.int32, ids.shape, 0)
            ids = jnp.where(slot < lens[f : f + 1], ids, -1)
            times = jnp.zeros(ids.shape, jnp.float32)
            for p in range(slots):
                times += jnp.where(ids == ids[p : p + 1], 1.0, 0.0)
            rows += [ids.astype(jnp.float32), times]
        tiles.append(jnp.concatenate(rows, axis=0))
    return tiles


def bag_columns(tiles, dest, block):
    per = LANES // block
    lane = lax.broadcasted_iota(jnp.int32, tiles[0].shape, 1) // block
    columns = []
    for first in range(0, len(tiles), per):
        merged = None
        for q in range(per):
            shift = lax.rem(q - dest + per, per) * block
            moved = pltpu.roll(tiles[first + q], shift, 1)
            merged = moved if merged is None else jnp.where(lane == q, moved, merged)
        pad = -merged.shape[0] % LANES
        if pad:
            merged = jnp.concatenate([merged, jnp.zeros((pad, LANES), jnp.float32)], axis=0)
        columns.append(merged.T)
    return columns


def pool_rows(columns, f, slots, table):
    rows, table_rows = columns.shape[0], table.shape[0]
    place = lax.broadcasted_iota(jnp.int16, (rows, table_rows), 1)
    counts = jnp.zeros((rows, table_rows), jnp.bfloat16)
    for p in range(slots):
        c = 2 * slots * f + p
        own = columns[:, c : c + 1].astype(jnp.int32).astype(jnp.int16)
        times = columns[:, c + slots : c + slots + 1].astype(jnp.bfloat16)
        counts = jnp.where(place == own, times, counts)
    return jnp.dot(counts, table, preferred_element_type=jnp.float32).astype(jnp.bfloat16)


def pool_dests(tiles, dests, block, slots, tables, buf, ready=None):
    feats, width = tables.shape[0], tables.shape[2]
    height = buf.shape[1]
    batch = max(1, BATCH // height)
    for first in range(0, len(dests), batch):
        some = dests[first : first + batch]
        columns = [c for d in some for c in bag_columns(tiles, d, block)]
        columns = jnp.concatenate(columns, axis=0) if len(columns) > 1 else columns[0]
        for f in range(feats):
            if ready is not None:
                ready(f)
            rows = pool_rows(columns, f, slots, tables[f])
            for i in range(len(some)):
                buf[first + i, :, f * width : (f + 1) * width] = rows[
                    i * height : (i + 1) * height
                ]


def first_kernel(
    k, block, towers, ids_hbm, len_hbm, tab_hbm, out_hbm, ids_ref, len_ref, tab_ref, buf, sems
):
    per = LANES // block
    feats, slots, _ = ids_ref.shape
    width = tab_ref.shape[2]
    bags = [
        pltpu.make_async_copy(ids_hbm, ids_ref, sems.at[0]),
        pltpu.make_async_copy(len_hbm, len_ref, sems.at[1]),
    ]
    rows = [
        pltpu.make_async_copy(tab_hbm.at[f], tab_ref.at[f], sems.at[2 + f]) for f in range(feats)
    ]
    for copy in bags + rows:
        copy.start()
    for copy in bags:
        copy.wait()
    tiles = bag_tiles(lax.axis_index("dev") // per ^ k // per, block, towers, ids_ref, len_ref)
    dest = lax.rem(lax.axis_index("dev"), per) ^ k % per
    columns = bag_columns(tiles, dest, block)
    columns = jnp.concatenate(columns, axis=0) if len(columns) > 1 else columns[0]
    sent = []
    for f in range(feats):
        rows[f].wait()
        at = pl.ds(f * width, width)
        buf[:, at] = pool_rows(columns, f, slots, tab_ref[f])
        sent.append(pltpu.make_async_copy(buf.at[:, at], out_hbm.at[:, at], sems.at[2 + feats + f]))
        sent[-1].start()
    for copy in sent:
        copy.wait()


def pool_first(ids, lens, tables, k, block, towers):
    feats = ids.shape[0]
    depth = feats * tables.shape[2]
    return pl.pallas_call(
        functools.partial(first_kernel, k, block, towers),
        in_specs=[ANY, ANY, ANY],
        out_specs=[ANY, VMEM, VMEM, VMEM],
        out_shape=[
            pltpu.HBM((towers * block, depth), jnp.bfloat16),
            jax.ShapeDtypeStruct(ids.shape, ids.dtype),
            jax.ShapeDtypeStruct(lens.shape, lens.dtype),
            jax.ShapeDtypeStruct(tables.shape, tables.dtype),
        ],
        scratch_shapes=[
            pltpu.VMEM((towers * block, depth), jnp.bfloat16),
            pltpu.SemaphoreType.DMA((2 + 2 * feats,)),
        ],
        compiler_params=pltpu.CompilerParams(vmem_limit_bytes=16 * MIB),
        name="pool_first",
    )(ids, lens, tables)


def more_kernel(ks, block, towers, ids_ref, len_ref, tab_ref, after_ref, *rest):
    outs, (buf, sems) = rest[:-2], rest[-2:]
    per = LANES // block
    slots = ids_ref.shape[1]
    low = lax.rem(lax.axis_index("dev"), per)
    for g in sorted({k // per for k in ks}):
        some = [i for i, k in enumerate(ks) if k // per == g]
        tiles = bag_tiles(lax.axis_index("dev") // per ^ g, block, towers, ids_ref, len_ref)
        dests = [low ^ ks[i] % per for i in some]
        pool_dests(
            tiles, dests, block, slots, tab_ref, buf.at[some[0] : some[0] + len(some)]
        )
    copies = [pltpu.make_async_copy(buf.at[i], out, sems.at[i]) for i, out in enumerate(outs)]
    for copy in copies:
        copy.start()
    for copy in copies:
        copy.wait()


def pool_more(ids, lens, tables, after, ks, block, towers):
    depth = ids.shape[0] * tables.shape[2]
    shape = (towers * block, depth)
    return pl.pallas_call(
        functools.partial(more_kernel, ks, block, towers),
        in_specs=[VMEM, VMEM, VMEM, ANY],
        out_specs=[ANY] * len(ks),
        out_shape=[pltpu.HBM(shape, jnp.bfloat16)] * len(ks),
        scratch_shapes=[
            pltpu.VMEM((len(ks),) + shape, jnp.bfloat16),
            pltpu.SemaphoreType.DMA((len(ks),)),
        ],
        compiler_params=pltpu.CompilerParams(vmem_limit_bytes=16 * MIB),
        cost_estimate=pl.CostEstimate(flops=10**9, bytes_accessed=0, transcendentals=0),
        name="pool_more",
    )(ids, lens, tables, after)


def low_kernel(ks, held, down_ref, *rest):
    chunks, low, out_ref = rest[: len(ks)], rest[len(ks) : -1 - held], rest[-1]
    depth = chunks[0].shape[1]
    total = low[0][...] if low else None
    for k, chunk in zip(ks, chunks, strict=True):
        at = pl.ds(pl.multiple_of((lax.axis_index("dev") ^ k) * depth, depth), depth)
        part = jnp.dot(chunk[...], down_ref[at, :], preferred_element_type=jnp.float32)
        total = part if total is None else total + part
    out_ref[...] = total


def low_part(down, chunks, ks, low, held=()):
    return pl.pallas_call(
        functools.partial(low_kernel, ks, len(held)),
        in_specs=[VMEM] * (1 + len(ks) + len(low)) + [ANY] * len(held),
        out_specs=VMEM,
        out_shape=jax.ShapeDtypeStruct((chunks[0].shape[0], down.shape[1]), jnp.float32),
        compiler_params=pltpu.CompilerParams(vmem_limit_bytes=16 * MIB),
        cost_estimate=pl.CostEstimate(flops=10**9, bytes_accessed=0, transcendentals=0),
        name="low_part",
    )(down, *chunks, *low, *held)


def tower_kernel(
    ks, late, towers, low_ref, down_ref, up_ref, bias_ref, proj_ref, pb_ref, *rest
):
    chunks, outs, scratch = rest[: -towers - 1], rest[-towers - 1 : -1], rest[-1]
    depth = chunks[0].shape[1]
    block = outs[0].shape[0]
    chunks = [
        (pl.ds(pl.multiple_of((lax.axis_index("dev") ^ k) * depth, depth), depth), chunk)
        for k, chunk in zip(ks, chunks, strict=True)
    ]
    low = low_ref[...]
    for at, chunk in chunks[-late:]:
        low += jnp.dot(chunk[...], down_ref[at, :], preferred_element_type=jnp.float32)
    low = low.astype(jnp.bfloat16)
    total = pb_ref[...]
    for at, chunk in chunks:
        high = jnp.dot(low, up_ref[:, at], preferred_element_type=jnp.float32)
        high = high + bias_ref[:, at]
        base = chunk[...].astype(jnp.float32)
        cross = (base * high + base).astype(jnp.bfloat16)
        total = total + jnp.dot(cross, proj_ref[at, :], preferred_element_type=jnp.float32)
    scratch[...] = total.astype(jnp.bfloat16)
    for k, out in enumerate(outs):
        out[...] = scratch[pl.ds(pl.multiple_of((lax.axis_index("tower") ^ k) * block, block), block), :]


def tower_out(low, down, up, bias, proj, pb, chunks, ks, late, towers):
    rows = chunks[0].shape[0]
    shape = jax.ShapeDtypeStruct((rows // towers, proj.shape[1]), jnp.bfloat16)
    return pl.pallas_call(
        functools.partial(tower_kernel, ks, late, towers),
        in_specs=[VMEM] * (6 + len(chunks)),
        out_specs=[VMEM] * towers,
        out_shape=[shape] * towers,
        scratch_shapes=[pltpu.VMEM((rows, proj.shape[1]), jnp.bfloat16)],
        compiler_params=pltpu.CompilerParams(vmem_limit_bytes=16 * MIB),
        cost_estimate=pl.CostEstimate(
            flops=4 * rows * proj.size, bytes_accessed=0, transcendentals=0
        ),
        name="tower_out",
    )(low, down, up, bias, proj, pb, *chunks)


def gram_kernel(*rest):
    chunks, out_ref, rows_ref = rest[:-2], rest[-2], rest[-1]
    towers, (block, width) = len(chunks), chunks[0].shape
    for k, chunk in enumerate(chunks):
        rows_ref[lax.axis_index("tower") ^ k] = chunk[...]
    rows = rows_ref[...].reshape(towers * block, width)
    gram = lax.dot_general(
        rows, rows, (((1,), (1,)), ((), ())), preferred_element_type=jnp.float32
    ) * (1.0 / np.sqrt(np.float32(width)))
    n = towers * block
    at = lax.broadcasted_iota(jnp.int32, (block, n), 0)
    to = lax.broadcasted_iota(jnp.int32, (block, n), 1)
    own = at == lax.rem(to, block)
    place = 0
    for i in range(towers):
        picked = jnp.where(own, gram[i * block : (i + 1) * block], 0.0)
        line = jnp.sum(picked, axis=0, keepdims=True)
        for j in range(i + 1, towers):
            out_ref[place : place + 1, :] = line[:, j * block : (j + 1) * block]
            place += 1


def gram_pairs(chunks):
    towers, (block, width) = len(chunks), chunks[0].shape
    pairs = towers * (towers - 1) // 2
    return pl.pallas_call(
        gram_kernel,
        in_specs=[VMEM] * towers,
        out_specs=VMEM,
        out_shape=jax.ShapeDtypeStruct((pairs, block), jnp.float32),
        scratch_shapes=[pltpu.VMEM((towers, block, width), jnp.bfloat16)],
        compiler_params=pltpu.CompilerParams(vmem_limit_bytes=16 * MIB),
        name="gram_pairs",
    )(*chunks)


def swap(x, axis, k):
    size = lax.axis_size(axis)
    return lax.ppermute(x, axis, [(i, i ^ k) for i in range(size)])


def local(bag_ids, bag_lengths, tables, cross_down, cross_up, cross_bias, proj_weight, proj_bias):
    towers = lax.axis_size("tower")
    members = lax.axis_size("dev")
    samples = bag_ids.shape[1]
    block = samples // (towers * members)
    per = LANES // block
    groups = members // per
    ids = bag_ids[0].transpose(1, 2, 0)
    lens = bag_lengths[0].transpose(1, 0)
    bias = cross_bias[0]
    fixed = [ids, lens, tables[0], cross_down[0, 0], cross_up[0, 0], proj_weight[0]]
    ids, lens, rows, *weights = (pltpu.with_memory_space_constraint(w, pltpu.HBM) for w in fixed)
    down, up, proj = (pltpu.with_memory_space_constraint(w, pltpu.VMEM) for w in weights)
    far, near = list(range(per, members)), list(range(per - 1, 0, -1))
    order = far[:1] + near[:1] + far[1:-1] + near[1:-1] + far[-1:] + near[-1:]
    pooled, got = {}, {}
    pooled[far[0]], ids, lens, rows = pool_first(ids, lens, rows, far[0], block, towers)

    def pool(ks, after):
        ks = sorted(ks)
        done = pltpu.with_memory_space_constraint(pooled[after], pltpu.HBM)
        parts = pool_more(ids, lens, rows, done, ks, block, towers)
        pooled.update(zip(ks, parts, strict=True))

    pool(order[1 : len(far)], far[0])
    pool([0] + order[len(far) :], far[-2])
    for k in order:
        got[k] = swap(pooled[k], "dev", k)
    got[0] = pooled[0]
    low = []
    for some in [[k] for k in order[: len(far)]] + [[0] + near[1:-1]]:
        held = (up, proj) if some == near[:1] else ()
        low = [low_part(down, [got[k] for k in some], some, low, held)]
    ks = [0] + order
    outs = tower_out(low[0], down, up, bias, proj, proj_bias, [got[k] for k in ks], ks, 2, towers)
    met = [outs[0]] + [swap(outs[k], "tower", k) for k in range(1, towers)]
    return gram_pairs(met).T


def solution(mesh):
    placed = (
        P("tower", None, "dev", None),
        P("tower", None, "dev"),
        P("tower", "dev", None, None),
        P("tower", None, None, None),
        P("tower", None, None, None),
        P("tower", None, None),
        P("tower", None, None),
        P("tower", None),
    )
    return jax.shard_map(
        local, mesh=mesh, in_specs=placed, out_specs=P(("tower", "dev"), None), check_vma=False
    )
```

```python
import functools

import jax
import jax.numpy as jnp
import numpy as np
from jax import lax
from jax.experimental import pallas as pl
from jax.experimental.pallas import tpu as pltpu
from jax.sharding import PartitionSpec as P

LANES = 128
MIB = 1 << 20
BATCH = 512
SPLIT = 256
ANY = pl.BlockSpec(memory_space=pl.ANY)
VMEM = pl.BlockSpec(memory_space=pltpu.VMEM)


def bag_tiles(group, block, towers, ids_ref, len_ref):
    feats, slots, samples = ids_ref.shape
    groups = samples // (towers * LANES)
    tiles = []
    for t in range(towers):
        at = pl.ds(pl.multiple_of((t * groups + group) * LANES, LANES), LANES)
        lens = len_ref[:, at]
        rows = []
        for f in range(feats):
            ids = ids_ref[f, :, at]
            slot = lax.broadcasted_iota(jnp.int32, ids.shape, 0)
            ids = jnp.where(slot < lens[f : f + 1], ids, -1)
            times = jnp.zeros(ids.shape, jnp.float32)
            for p in range(slots):
                times += jnp.where(ids == ids[p : p + 1], 1.0, 0.0)
            rows += [ids.astype(jnp.float32), times]
        tiles.append(jnp.concatenate(rows, axis=0))
    return tiles


def bag_columns(tiles, dest, block):
    per = LANES // block
    lane = lax.broadcasted_iota(jnp.int32, tiles[0].shape, 1) // block
    columns = []
    for first in range(0, len(tiles), per):
        merged = None
        for q in range(per):
            shift = lax.rem(q - dest + per, per) * block
            moved = pltpu.roll(tiles[first + q], shift, 1)
            merged = moved if merged is None else jnp.where(lane == q, moved, merged)
        pad = -merged.shape[0] % LANES
        if pad:
            merged = jnp.concatenate([merged, jnp.zeros((pad, LANES), jnp.float32)], axis=0)
        columns.append(merged.T)
    return columns


def pool_rows(columns, f, slots, table):
    rows, table_rows = columns.shape[0], table.shape[0]
    place = lax.broadcasted_iota(jnp.int16, (rows, table_rows), 1)
    counts = jnp.zeros((rows, table_rows), jnp.bfloat16)
    for p in range(slots):
        c = 2 * slots * f + p
        own = columns[:, c : c + 1].astype(jnp.int32).astype(jnp.int16)
        times = columns[:, c + slots : c + slots + 1].astype(jnp.bfloat16)
        counts = jnp.where(place == own, times, counts)
    return jnp.dot(counts, table, preferred_element_type=jnp.float32).astype(jnp.bfloat16)


def pool_dests(tiles, dests, block, slots, tables, buf, ready=None):
    feats, width = tables.shape[0], tables.shape[2]
    height = buf.shape[1]
    batch = max(1, BATCH // height)
    for first in range(0, len(dests), batch):
        some = dests[first : first + batch]
        columns = [c for d in some for c in bag_columns(tiles, d, block)]
        columns = jnp.concatenate(columns, axis=0) if len(columns) > 1 else columns[0]
        for f in range(feats):
            if ready is not None:
                ready(f)
            rows = pool_rows(columns, f, slots, tables[f])
            for i in range(len(some)):
                buf[first + i, :, f * width : (f + 1) * width] = rows[
                    i * height : (i + 1) * height
                ]


def first_kernel(
    k, block, towers, ids_hbm, len_hbm, tab_hbm, out_ref, ids_ref, len_ref, tab_ref, sems
):
    per = LANES // block
    feats, slots, _ = ids_ref.shape
    width = tab_ref.shape[2]
    bags = [
        pltpu.make_async_copy(ids_hbm, ids_ref, sems.at[0]),
        pltpu.make_async_copy(len_hbm, len_ref, sems.at[1]),
    ]
    rows = [
        pltpu.make_async_copy(tab_hbm.at[f], tab_ref.at[f], sems.at[2 + f]) for f in range(feats)
    ]
    for copy in bags + rows:
        copy.start()
    for copy in bags:
        copy.wait()
    tiles = bag_tiles(lax.axis_index("dev") // per ^ k // per, block, towers, ids_ref, len_ref)
    dest = lax.rem(lax.axis_index("dev"), per) ^ k % per
    columns = bag_columns(tiles, dest, block)
    columns = jnp.concatenate(columns, axis=0) if len(columns) > 1 else columns[0]
    for f in range(feats):
        rows[f].wait()
        out_ref[:, f * width : (f + 1) * width] = pool_rows(columns, f, slots, tab_ref[f])


def pool_first(ids, lens, tables, k, block, towers):
    feats = ids.shape[0]
    depth = feats * tables.shape[2]
    return pl.pallas_call(
        functools.partial(first_kernel, k, block, towers),
        in_specs=[ANY, ANY, ANY],
        out_specs=[VMEM, VMEM, VMEM, VMEM],
        out_shape=[
            pltpu.VMEM((towers * block, depth), jnp.bfloat16),
            jax.ShapeDtypeStruct(ids.shape, ids.dtype),
            jax.ShapeDtypeStruct(lens.shape, lens.dtype),
            jax.ShapeDtypeStruct(tables.shape, tables.dtype),
        ],
        scratch_shapes=[pltpu.SemaphoreType.DMA((2 + feats,))],
        compiler_params=pltpu.CompilerParams(vmem_limit_bytes=16 * MIB),
        name="pool_first",
    )(ids, lens, tables)


def more_kernel(ks, block, towers, ids_ref, len_ref, tab_ref, after_ref, *rest):
    outs, (buf, sems) = rest[:-2], rest[-2:]
    per = LANES // block
    slots = ids_ref.shape[1]
    low = lax.rem(lax.axis_index("dev"), per)
    for g in sorted({k // per for k in ks}):
        some = [i for i, k in enumerate(ks) if k // per == g]
        tiles = bag_tiles(lax.axis_index("dev") // per ^ g, block, towers, ids_ref, len_ref)
        dests = [low ^ ks[i] % per for i in some]
        pool_dests(
            tiles, dests, block, slots, tab_ref, buf.at[some[0] : some[0] + len(some)]
        )
    copies = [pltpu.make_async_copy(buf.at[i], out, sems.at[i]) for i, out in enumerate(outs)]
    for copy in copies:
        copy.start()
    for copy in copies:
        copy.wait()


def pool_more(ids, lens, tables, after, ks, block, towers):
    depth = ids.shape[0] * tables.shape[2]
    shape = (towers * block, depth)
    return pl.pallas_call(
        functools.partial(more_kernel, ks, block, towers),
        in_specs=[VMEM, VMEM, VMEM, ANY],
        out_specs=[ANY] * len(ks),
        out_shape=[pltpu.HBM(shape, jnp.bfloat16)] * len(ks),
        scratch_shapes=[
            pltpu.VMEM((len(ks),) + shape, jnp.bfloat16),
            pltpu.SemaphoreType.DMA((len(ks),)),
        ],
        compiler_params=pltpu.CompilerParams(vmem_limit_bytes=16 * MIB),
        cost_estimate=pl.CostEstimate(flops=10**9, bytes_accessed=0, transcendentals=0),
        name="pool_more",
    )(ids, lens, tables, after)


def low_kernel(ks, held, down_ref, *rest):
    chunks, low, out_ref = rest[: len(ks)], rest[len(ks) : -1 - held], rest[-1]
    depth = chunks[0].shape[1]
    total = low[0][...] if low else None
    for k, chunk in zip(ks, chunks, strict=True):
        at = pl.ds(pl.multiple_of((lax.axis_index("dev") ^ k) * depth, depth), depth)
        part = jnp.dot(chunk[...], down_ref[at, :], preferred_element_type=jnp.float32)
        total = part if total is None else total + part
    out_ref[...] = total


def low_part(down, chunks, ks, low, held=()):
    return pl.pallas_call(
        functools.partial(low_kernel, ks, len(held)),
        in_specs=[VMEM] * (1 + len(ks) + len(low)) + [ANY] * len(held),
        out_specs=VMEM,
        out_shape=jax.ShapeDtypeStruct((chunks[0].shape[0], down.shape[1]), jnp.float32),
        compiler_params=pltpu.CompilerParams(vmem_limit_bytes=16 * MIB),
        cost_estimate=pl.CostEstimate(flops=10**9, bytes_accessed=0, transcendentals=0),
        name="low_part",
    )(down, *chunks, *low, *held)


def tower_kernel(
    ks, late, towers, low_ref, down_ref, up_ref, bias_ref, proj_ref, pb_ref, *rest
):
    chunks, outs, scratch = rest[: -towers - 1], rest[-towers - 1 : -1], rest[-1]
    depth = chunks[0].shape[1]
    block = outs[0].shape[0]
    low = low_ref[...]
    for k, chunk in list(zip(ks, chunks, strict=True))[-late:]:
        at = pl.ds(pl.multiple_of((lax.axis_index("dev") ^ k) * depth, depth), depth)
        low += jnp.dot(chunk[...], down_ref[at, :], preferred_element_type=jnp.float32)
    low = low.astype(jnp.bfloat16)
    total = pb_ref[...]
    for k, chunk in zip(ks, chunks, strict=True):
        for first in range(0, depth, SPLIT):
            start = (lax.axis_index("dev") ^ k) * depth + first
            at = pl.ds(pl.multiple_of(start, SPLIT), SPLIT)
            high = jnp.dot(low, up_ref[:, at], preferred_element_type=jnp.float32)
            high = high + bias_ref[:, at]
            base = chunk[:, first : first + SPLIT].astype(jnp.float32)
            cross = (base * high + base).astype(jnp.bfloat16)
            total = total + jnp.dot(cross, proj_ref[at, :], preferred_element_type=jnp.float32)
    scratch[...] = total.astype(jnp.bfloat16)
    for k, out in enumerate(outs):
        out[...] = scratch[pl.ds(pl.multiple_of((lax.axis_index("tower") ^ k) * block, block), block), :]


def tower_out(low, down, up, bias, proj, pb, chunks, ks, late, towers):
    rows = chunks[0].shape[0]
    shape = jax.ShapeDtypeStruct((rows // towers, proj.shape[1]), jnp.bfloat16)
    return pl.pallas_call(
        functools.partial(tower_kernel, ks, late, towers),
        in_specs=[VMEM] * (6 + len(chunks)),
        out_specs=[VMEM] * towers,
        out_shape=[shape] + [pltpu.VMEM(shape.shape, shape.dtype)] * (towers - 1),
        scratch_shapes=[pltpu.VMEM((rows, proj.shape[1]), jnp.bfloat16)],
        compiler_params=pltpu.CompilerParams(vmem_limit_bytes=16 * MIB),
        cost_estimate=pl.CostEstimate(
            flops=4 * rows * proj.size, bytes_accessed=0, transcendentals=0
        ),
        name="tower_out",
    )(low, down, up, bias, proj, pb, *chunks)


def gram_kernel(*rest):
    chunks, out_ref, rows_ref = rest[:-2], rest[-2], rest[-1]
    towers, (block, width) = len(chunks), chunks[0].shape
    for k, chunk in enumerate(chunks):
        rows_ref[lax.axis_index("tower") ^ k] = chunk[...]
    rows = rows_ref[...].reshape(towers * block, width)
    gram = lax.dot_general(
        rows, rows, (((1,), (1,)), ((), ())), preferred_element_type=jnp.float32
    ) * (1.0 / np.sqrt(np.float32(width)))
    n = towers * block
    at = lax.broadcasted_iota(jnp.int32, (block, n), 0)
    to = lax.broadcasted_iota(jnp.int32, (block, n), 1)
    own = at == lax.rem(to, block)
    place = 0
    for i in range(towers):
        picked = jnp.where(own, gram[i * block : (i + 1) * block], 0.0)
        line = jnp.sum(picked, axis=0, keepdims=True)
        for j in range(i + 1, towers):
            out_ref[place : place + 1, :] = line[:, j * block : (j + 1) * block]
            place += 1


def gram_pairs(chunks):
    towers, (block, width) = len(chunks), chunks[0].shape
    pairs = towers * (towers - 1) // 2
    return pl.pallas_call(
        gram_kernel,
        in_specs=[VMEM] * towers,
        out_specs=VMEM,
        out_shape=jax.ShapeDtypeStruct((pairs, block), jnp.float32),
        scratch_shapes=[pltpu.VMEM((towers, block, width), jnp.bfloat16)],
        compiler_params=pltpu.CompilerParams(vmem_limit_bytes=16 * MIB),
        name="gram_pairs",
    )(*chunks)


def swap(x, axis, k):
    size = lax.axis_size(axis)
    return lax.ppermute(x, axis, [(i, i ^ k) for i in range(size)])


def local(bag_ids, bag_lengths, tables, cross_down, cross_up, cross_bias, proj_weight, proj_bias):
    towers = lax.axis_size("tower")
    members = lax.axis_size("dev")
    samples = bag_ids.shape[1]
    block = samples // (towers * members)
    per = LANES // block
    groups = members // per
    ids = bag_ids[0].transpose(1, 2, 0)
    lens = bag_lengths[0].transpose(1, 0)
    bias = cross_bias[0]
    fixed = [ids, lens, tables[0], cross_down[0, 0], cross_up[0, 0], proj_weight[0]]
    ids, lens, rows, *weights = (pltpu.with_memory_space_constraint(w, pltpu.HBM) for w in fixed)
    down, up, proj = (pltpu.with_memory_space_constraint(w, pltpu.VMEM) for w in weights)
    far, near = list(range(per, members)), [1] + list(range(per - 1, 1, -1))
    order = far[:1] + near[:1] + far[1:-1] + near[1:-1] + far[-1:] + near[-1:]
    pooled, got = {}, {}
    pooled[far[0]], ids, lens, rows = pool_first(ids, lens, rows, far[0], block, towers)

    def pool(ks, after):
        ks = sorted(ks)
        done = pltpu.with_memory_space_constraint(pooled[after], pltpu.HBM)
        parts = pool_more(ids, lens, rows, done, ks, block, towers)
        pooled.update(zip(ks, parts, strict=True))

    pool(order[1 : len(far)], far[0])
    pool([0] + order[len(far) :], far[-2])
    for k in order:
        got[k] = swap(pooled[k], "dev", k)
    got[0] = pooled[0]
    low = []
    for i, some in enumerate([far[:1],near[:1],far[1:-1]+[0]+near[1:-1]]):
        held = (up, proj) if i == 1 else ()
        low = [low_part(down, [got[k] for k in some], some, low, held)]
    ks = [0] + order
    outs = tower_out(low[0], down, up, bias, proj, proj_bias, [got[k] for k in ks], ks, 2, towers)
    met = [outs[0]] + [swap(outs[k], "tower", k) for k in range(1, towers)]
    return gram_pairs(met).T


def solution(mesh):
    placed = (
        P("tower", None, "dev", None),
        P("tower", None, "dev"),
        P("tower", "dev", None, None),
        P("tower", None, None, None),
        P("tower", None, None, None),
        P("tower", None, None),
        P("tower", None, None),
        P("tower", None),
    )
    return jax.shard_map(
        local, mesh=mesh, in_specs=placed, out_specs=P(("tower", "dev"), None), check_vma=False
    )
```

```python
import functools

import jax
import jax.numpy as jnp
import numpy as np
from jax import lax
from jax.experimental import pallas as pl
from jax.experimental.pallas import tpu as pltpu
from jax.sharding import PartitionSpec as P

LANES = 128
MIB = 1 << 20
BATCH = 512
SPLIT = 256
ANY = pl.BlockSpec(memory_space=pl.ANY)
VMEM = pl.BlockSpec(memory_space=pltpu.VMEM)


def bag_columns(group, dest, block, towers, ids_ref, len_ref):
    feats, slots, samples = ids_ref.shape
    groups, per = samples // (towers * LANES), LANES // block
    lane = lax.broadcasted_iota(jnp.int32, (feats * slots, LANES), 1) // block
    columns = []
    for first in range(0, towers, per):
        bags = lens = None
        for q in range(per):
            start = ((first + q) * groups + group) * LANES
            at = pl.ds(pl.multiple_of(start, LANES), LANES)
            shift = lax.rem(q - dest + per, per) * block
            ids = jnp.concatenate([ids_ref[f, :, at] for f in range(feats)], axis=0)
            ids, own = pltpu.roll(ids, shift, 1), pltpu.roll(len_ref[:, at], shift, 1)
            bags = ids if bags is None else jnp.where(lane == q, ids, bags)
            lens = own if lens is None else jnp.where(lane[:feats] == q, own, lens)
        rows = []
        for f in range(feats):
            ids = bags[f * slots : (f + 1) * slots]
            slot = lax.broadcasted_iota(jnp.int32, ids.shape, 0)
            ids = jnp.where(slot < lens[f : f + 1], ids, -1)
            times = jnp.zeros(ids.shape, jnp.float32)
            for p in range(slots):
                times += jnp.where(ids == ids[p : p + 1], 1.0, 0.0)
            rows += [ids.astype(jnp.float32), times]
        rows = jnp.concatenate(rows, axis=0)
        columns.append(rows.T)
    return columns


def pool_rows(columns, f, slots, table):
    rows, table_rows = columns.shape[0], table.shape[0]
    place = lax.broadcasted_iota(jnp.int16, (rows, table_rows), 1)
    counts = jnp.zeros((rows, table_rows), jnp.bfloat16)
    for p in range(slots):
        c = 2 * slots * f + p
        own = columns[:, c : c + 1].astype(jnp.int32).astype(jnp.int16)
        times = columns[:, c + slots : c + slots + 1].astype(jnp.bfloat16)
        counts = jnp.where(place == own, times, counts)
    return jnp.dot(counts, table, preferred_element_type=jnp.float32).astype(jnp.bfloat16)


def pool_dests(group, dests, block, towers, ids_ref, len_ref, tables, outs, ready):
    (feats, slots, _), width = ids_ref.shape, tables.shape[2]
    height = outs[0].shape[0]
    batch = max(1, BATCH // height)
    for first in range(0, len(dests), batch):
        some = dests[first : first + batch]
        columns = [
            c for d in some for c in bag_columns(group, d, block, towers, ids_ref, len_ref)
        ]
        columns = jnp.concatenate(columns, axis=0) if len(columns) > 1 else columns[0]
        for f in range(feats):
            if ready is not None and first == 0:
                ready[f].wait()
            rows = pool_rows(columns, f, slots, tables[f])
            for i in range(len(some)):
                outs[first + i][:, f * width : (f + 1) * width] = rows[
                    i * height : (i + 1) * height
                ]


def pool_groups(ks, block, towers, ids_ref, len_ref, tab_ref, outs, ready=None):
    per = LANES // block
    me = lax.axis_index("dev")
    for g in sorted({k // per for k in ks}):
        some = [i for i, k in enumerate(ks) if k // per == g]
        dests = [lax.rem(me, per) ^ ks[i] % per for i in some]
        some = [outs[i] for i in some]
        pool_dests(me // per ^ g, dests, block, towers, ids_ref, len_ref, tab_ref, some, ready)
        ready = None


def first_kernel(ks, block, towers, ids_hbm, len_hbm, tab_hbm, ids_ref, len_ref, tab_ref, *rest):
    outs, sems = rest[:-1], rest[-1]
    feats = ids_ref.shape[0]
    bags = [
        pltpu.make_async_copy(ids_hbm, ids_ref, sems.at[0]),
        pltpu.make_async_copy(len_hbm, len_ref, sems.at[1]),
    ]
    rows = [
        pltpu.make_async_copy(tab_hbm.at[f], tab_ref.at[f], sems.at[2 + f]) for f in range(feats)
    ]
    for copy in bags + rows:
        copy.start()
    for copy in bags:
        copy.wait()
    pool_groups(ks, block, towers, ids_ref, len_ref, tab_ref, outs, rows)


def pool_first(ids, lens, tables, ks, block, towers):
    feats = ids.shape[0]
    shape = (towers * block, feats * tables.shape[2])
    return pl.pallas_call(
        functools.partial(first_kernel, ks, block, towers),
        in_specs=[ANY] * 3,
        out_specs=[VMEM] * (3 + len(ks)),
        out_shape=[jax.ShapeDtypeStruct(x.shape, x.dtype) for x in (ids, lens, tables)]
        + [pltpu.VMEM(shape, jnp.bfloat16)] * len(ks),
        scratch_shapes=[pltpu.SemaphoreType.DMA((2 + feats,))],
        compiler_params=pltpu.CompilerParams(vmem_limit_bytes=16 * MIB),
        name="pool_first",
    )(ids, lens, tables)


def more_kernel(ks, block, towers, ids_ref, len_ref, tab_ref, after_ref, *outs):
    pool_groups(ks, block, towers, ids_ref, len_ref, tab_ref, outs)


def pool_more(ids, lens, tables, after, ks, block, towers):
    shape = (towers * block, ids.shape[0] * tables.shape[2])
    return pl.pallas_call(
        functools.partial(more_kernel, ks, block, towers),
        in_specs=[VMEM, VMEM, VMEM, ANY],
        out_specs=[VMEM] * len(ks),
        out_shape=[pltpu.VMEM(shape, jnp.bfloat16)] * len(ks),
        compiler_params=pltpu.CompilerParams(vmem_limit_bytes=16 * MIB),
        cost_estimate=pl.CostEstimate(flops=2 * 10**9, bytes_accessed=0, transcendentals=0),
        name="pool_more",
    )(ids, lens, tables, after)


def low_kernel(ks, held, down_ref, *rest):
    chunks, low, out_ref = rest[: len(ks)], rest[len(ks) : -1 - held], rest[-1]
    depth = chunks[0].shape[1]
    total = low[0][...] if low else None
    for k, chunk in zip(ks, chunks, strict=True):
        at = pl.ds(pl.multiple_of((lax.axis_index("dev") ^ k) * depth, depth), depth)
        part = jnp.dot(chunk[...], down_ref[at, :], preferred_element_type=jnp.float32)
        total = part if total is None else total + part
    out_ref[...] = total


def low_part(down, chunks, ks, low, held=()):
    return pl.pallas_call(
        functools.partial(low_kernel, ks, len(held)),
        in_specs=[VMEM] * (1 + len(ks) + len(low)) + [ANY] * len(held),
        out_specs=VMEM,
        out_shape=jax.ShapeDtypeStruct((chunks[0].shape[0], down.shape[1]), jnp.float32),
        compiler_params=pltpu.CompilerParams(vmem_limit_bytes=16 * MIB),
        cost_estimate=pl.CostEstimate(flops=4 * 10**9, bytes_accessed=0, transcendentals=0),
        name="low_part",
    )(down, *chunks, *low, *held)


def tower_kernel(
    ks, late, towers, low_ref, down_ref, up_ref, bias_ref, proj_ref, pb_ref, *rest
):
    chunks, outs, scratch = rest[: -towers - 1], rest[-towers - 1 : -1], rest[-1]
    depth = chunks[0].shape[1]
    block = outs[0].shape[0]
    low = low_ref[...]
    for k, chunk in list(zip(ks, chunks, strict=True))[-late:]:
        at = pl.ds(pl.multiple_of((lax.axis_index("dev") ^ k) * depth, depth), depth)
        low += jnp.dot(chunk[...], down_ref[at, :], preferred_element_type=jnp.float32)
    low = low.astype(jnp.bfloat16)
    total = pb_ref[...]
    for k, chunk in zip(ks, chunks, strict=True):
        for first in range(0, depth, SPLIT):
            start = (lax.axis_index("dev") ^ k) * depth + first
            at = pl.ds(pl.multiple_of(start, SPLIT), SPLIT)
            high = jnp.dot(low, up_ref[:, at], preferred_element_type=jnp.float32)
            high = high + bias_ref[:, at]
            base = chunk[:, first : first + SPLIT].astype(jnp.float32)
            cross = (base * high + base).astype(jnp.bfloat16)
            total = total + jnp.dot(cross, proj_ref[at, :], preferred_element_type=jnp.float32)
    scratch[...] = total.astype(jnp.bfloat16)
    for k, out in enumerate(outs):
        out[...] = scratch[pl.ds(pl.multiple_of((lax.axis_index("tower") ^ k) * block, block), block), :]


def tower_out(low, down, up, bias, proj, pb, chunks, ks, late, towers):
    rows = chunks[0].shape[0]
    shape = jax.ShapeDtypeStruct((rows // towers, proj.shape[1]), jnp.bfloat16)
    return pl.pallas_call(
        functools.partial(tower_kernel, ks, late, towers),
        in_specs=[VMEM] * (6 + len(chunks)),
        out_specs=[VMEM] * towers,
        out_shape=[shape] + [pltpu.VMEM(shape.shape, shape.dtype)] * (towers - 1),
        scratch_shapes=[pltpu.VMEM((rows, proj.shape[1]), jnp.bfloat16)],
        compiler_params=pltpu.CompilerParams(vmem_limit_bytes=16 * MIB),
        cost_estimate=pl.CostEstimate(
            flops=4 * rows * proj.size, bytes_accessed=0, transcendentals=0
        ),
        name="tower_out",
    )(low, down, up, bias, proj, pb, *chunks)


def gram_kernel(*rest):
    chunks, out_ref, rows_ref = rest[:-2], rest[-2], rest[-1]
    towers, (block, width) = len(chunks), chunks[0].shape
    for k, chunk in enumerate(chunks):
        rows_ref[lax.axis_index("tower") ^ k] = chunk[...]
    rows = rows_ref[...].reshape(towers * block, width)
    gram = lax.dot_general(
        rows, rows, (((1,), (1,)), ((), ())), preferred_element_type=jnp.float32
    ) * (1.0 / np.sqrt(np.float32(width)))
    n = towers * block
    at = lax.broadcasted_iota(jnp.int32, (block, n), 0)
    to = lax.broadcasted_iota(jnp.int32, (block, n), 1)
    own = at == lax.rem(to, block)
    place = 0
    for i in range(towers):
        picked = jnp.where(own, gram[i * block : (i + 1) * block], 0.0)
        line = jnp.sum(picked, axis=0, keepdims=True)
        for j in range(i + 1, towers):
            out_ref[place : place + 1, :] = line[:, j * block : (j + 1) * block]
            place += 1


def gram_pairs(chunks):
    towers, (block, width) = len(chunks), chunks[0].shape
    pairs = towers * (towers - 1) // 2
    return pl.pallas_call(
        gram_kernel,
        in_specs=[VMEM] * towers,
        out_specs=VMEM,
        out_shape=jax.ShapeDtypeStruct((pairs, block), jnp.float32),
        scratch_shapes=[pltpu.VMEM((towers, block, width), jnp.bfloat16)],
        compiler_params=pltpu.CompilerParams(vmem_limit_bytes=16 * MIB),
        name="gram_pairs",
    )(*chunks)


def swap(x, axis, k):
    size = lax.axis_size(axis)
    return lax.ppermute(x, axis, [(i, i ^ k) for i in range(size)])


def local(bag_ids, bag_lengths, tables, cross_down, cross_up, cross_bias, proj_weight, proj_bias):
    towers = lax.axis_size("tower")
    members = lax.axis_size("dev")
    samples = bag_ids.shape[1]
    block = samples // (towers * members)
    per = LANES // block
    groups = members // per
    ids = bag_ids[0].transpose(1, 2, 0)
    lens = bag_lengths[0].transpose(1, 0)
    bias = cross_bias[0]
    fixed = [ids, lens, tables[0], cross_down[0, 0], cross_up[0, 0], proj_weight[0]]
    ids, lens, rows, *weights = (pltpu.with_memory_space_constraint(w, pltpu.HBM) for w in fixed)
    down, up, proj = (pltpu.with_memory_space_constraint(w, pltpu.VMEM) for w in weights)
    far, near = list(range(per, members)), [1] + list(range(per - 1, 1, -1))
    order = far[:1] + near[:1] + far[1:-1] + near[1:-1] + far[-1:] + near[-1:]
    batches = [
        far[:1],
        [0] + near[:1] + far[1:2],
        near[1:-1] + far[2:-1],
        near[-1:] + far[-1:],
    ]
    steps = [far[:1], near[:1], far[1:-1] + [0] + near[1:-1]]
    pooled, got = {}, {}
    ids, lens, rows, *parts = pool_first(ids, lens, rows, batches[0], block, towers)
    pooled.update(zip(batches[0], parts, strict=True))
    for ks in batches[1:]:
        after = pltpu.with_memory_space_constraint(parts[0], pltpu.VMEM)
        parts = pool_more(ids, lens, rows, after, ks, block, towers)
        pooled.update(zip(ks, parts, strict=True))
    for k in order:
        got[k] = swap(pooled[k], "dev", k)
    got[0] = pooled[0]
    low = []
    for i, some in enumerate(steps):
        held = (up, proj) if i == 1 else ()
        low = [low_part(down, [got[k] for k in some], some, low, held)]
    done = [k for some in steps for k in some]
    ks = done + [k for k in [0] + order if k not in done]
    outs = tower_out(low[0], down, up, bias, proj, proj_bias, [got[k] for k in ks], ks, len(ks) - len(done), towers)
    met = [outs[0]] + [swap(outs[k], "tower", k) for k in range(1, towers)]
    return gram_pairs(met).T


def solution(mesh):
    placed = (
        P("tower", None, "dev", None),
        P("tower", None, "dev"),
        P("tower", "dev", None, None),
        P("tower", None, None, None),
        P("tower", None, None, None),
        P("tower", None, None),
        P("tower", None, None),
        P("tower", None),
    )
    return jax.shard_map(
        local, mesh=mesh, in_specs=placed, out_specs=P(("tower", "dev"), None), check_vma=False
    )
```

```python
import functools

import jax
import jax.numpy as jnp
import numpy as np
from jax import lax
from jax.experimental import pallas as pl
from jax.experimental.pallas import tpu as pltpu
from jax.sharding import PartitionSpec as P

LANES = 128
MIB = 1 << 20
BATCH = 512
SPLIT = 256
ANY = pl.BlockSpec(memory_space=pl.ANY)
VMEM = pl.BlockSpec(memory_space=pltpu.VMEM)


def bag_columns(group, dest, block, towers, ids_ref, len_ref):
    feats, slots, samples = ids_ref.shape
    groups, per = samples // (towers * LANES), LANES // block
    lane = lax.broadcasted_iota(jnp.int32, (feats * slots, LANES), 1) // block
    columns = []
    for first in range(0, towers, per):
        bags = lens = None
        for q in range(per):
            start = ((first + q) * groups + group) * LANES
            at = pl.ds(pl.multiple_of(start, LANES), LANES)
            shift = lax.rem(q - dest + per, per) * block
            ids = jnp.concatenate([ids_ref[f, :, at] for f in range(feats)], axis=0)
            ids, own = pltpu.roll(ids, shift, 1), pltpu.roll(len_ref[:, at], shift, 1)
            bags = ids if bags is None else jnp.where(lane == q, ids, bags)
            lens = own if lens is None else jnp.where(lane[:feats] == q, own, lens)
        rows = []
        for f in range(feats):
            ids = bags[f * slots : (f + 1) * slots]
            slot = lax.broadcasted_iota(jnp.int32, ids.shape, 0)
            ids = jnp.where(slot < lens[f : f + 1], ids, -1)
            times = jnp.zeros(ids.shape, jnp.float32)
            for p in range(slots):
                times += jnp.where(ids == ids[p : p + 1], 1.0, 0.0)
            rows += [ids.astype(jnp.float32), times]
        rows = jnp.concatenate(rows, axis=0)
        columns.append(rows.T)
    return columns


def pool_rows(columns, f, slots, table):
    rows, table_rows = columns.shape[0], table.shape[0]
    place = lax.broadcasted_iota(jnp.int16, (rows, table_rows), 1)
    counts = jnp.zeros((rows, table_rows), jnp.bfloat16)
    for p in range(slots):
        c = 2 * slots * f + p
        own = columns[:, c : c + 1].astype(jnp.int32).astype(jnp.int16)
        times = columns[:, c + slots : c + slots + 1].astype(jnp.bfloat16)
        counts = jnp.where(place == own, times, counts)
    return jnp.dot(counts, table, preferred_element_type=jnp.float32).astype(jnp.bfloat16)


def pool_dests(group, dests, block, towers, ids_ref, len_ref, tables, outs, ready):
    (feats, slots, _), width = ids_ref.shape, tables.shape[2]
    height = outs[0].shape[0]
    batch = max(1, BATCH // height)
    for first in range(0, len(dests), batch):
        some = dests[first : first + batch]
        columns = [
            c for d in some for c in bag_columns(group, d, block, towers, ids_ref, len_ref)
        ]
        columns = jnp.concatenate(columns, axis=0) if len(columns) > 1 else columns[0]
        for f in range(feats):
            if ready is not None and first == 0:
                ready[f].wait()
            rows = pool_rows(columns, f, slots, tables[f])
            for i in range(len(some)):
                outs[first + i][:, f * width : (f + 1) * width] = rows[
                    i * height : (i + 1) * height
                ]


def pool_groups(ks, block, towers, ids_ref, len_ref, tab_ref, outs, ready=None):
    per = LANES // block
    me = lax.axis_index("dev")
    for g in sorted({k // per for k in ks}):
        some = [i for i, k in enumerate(ks) if k // per == g]
        dests = [lax.rem(me, per) ^ ks[i] % per for i in some]
        some = [outs[i] for i in some]
        pool_dests(me // per ^ g, dests, block, towers, ids_ref, len_ref, tab_ref, some, ready)
        ready = None


def first_kernel(ks, block, towers, ids_hbm, len_hbm, tab_hbm, ids_ref, len_ref, tab_ref, *rest):
    outs, sems = rest[:-1], rest[-1]
    feats = ids_ref.shape[0]
    bags = [
        pltpu.make_async_copy(ids_hbm, ids_ref, sems.at[0]),
        pltpu.make_async_copy(len_hbm, len_ref, sems.at[1]),
    ]
    rows = [
        pltpu.make_async_copy(tab_hbm.at[f], tab_ref.at[f], sems.at[2 + f]) for f in range(feats)
    ]
    for copy in bags + rows:
        copy.start()
    for copy in bags:
        copy.wait()
    pool_groups(ks, block, towers, ids_ref, len_ref, tab_ref, outs, rows)


def pool_first(ids, lens, tables, ks, block, towers):
    feats = ids.shape[0]
    shape = (towers * block, feats * tables.shape[2])
    return pl.pallas_call(
        functools.partial(first_kernel, ks, block, towers),
        in_specs=[ANY] * 3,
        out_specs=[VMEM] * (3 + len(ks)),
        out_shape=[jax.ShapeDtypeStruct(x.shape, x.dtype) for x in (ids, lens, tables)]
        + [pltpu.VMEM(shape, jnp.bfloat16)] * len(ks),
        scratch_shapes=[pltpu.SemaphoreType.DMA((2 + feats,))],
        compiler_params=pltpu.CompilerParams(vmem_limit_bytes=16 * MIB),
        name="pool_first",
    )(ids, lens, tables)


def more_kernel(ks, block, towers, ids_ref, len_ref, tab_ref, after_ref, *outs):
    pool_groups(ks, block, towers, ids_ref, len_ref, tab_ref, outs)


def pool_more(ids, lens, tables, after, ks, block, towers):
    shape = (towers * block, ids.shape[0] * tables.shape[2])
    return pl.pallas_call(
        functools.partial(more_kernel, ks, block, towers),
        in_specs=[VMEM, VMEM, VMEM, ANY],
        out_specs=[VMEM] * len(ks),
        out_shape=[pltpu.VMEM(shape, jnp.bfloat16)] * len(ks),
        compiler_params=pltpu.CompilerParams(vmem_limit_bytes=16 * MIB),
        cost_estimate=pl.CostEstimate(flops=2 * 10**9, bytes_accessed=0, transcendentals=0),
        name="pool_more",
    )(ids, lens, tables, after)


def low_kernel(ks, held, down_ref, *rest):
    chunks, low, out_ref = rest[: len(ks)], rest[len(ks) : -1 - held], rest[-1]
    depth = chunks[0].shape[1]
    total = low[0][...] if low else None
    for k, chunk in zip(ks, chunks, strict=True):
        at = pl.ds(pl.multiple_of((lax.axis_index("dev") ^ k) * depth, depth), depth)
        part = jnp.dot(chunk[...], down_ref[at, :], preferred_element_type=jnp.float32)
        total = part if total is None else total + part
    out_ref[...] = total


def low_part(down, chunks, ks, low, held=()):
    return pl.pallas_call(
        functools.partial(low_kernel, ks, len(held)),
        in_specs=[VMEM] * (1 + len(ks) + len(low)) + [ANY] * len(held),
        out_specs=VMEM,
        out_shape=jax.ShapeDtypeStruct((chunks[0].shape[0], down.shape[1]), jnp.float32),
        compiler_params=pltpu.CompilerParams(vmem_limit_bytes=16 * MIB),
        cost_estimate=pl.CostEstimate(flops=4 * 10**9, bytes_accessed=0, transcendentals=0),
        name="low_part",
    )(down, *chunks, *low, *held)


def tower_kernel(
    ks, late, towers, low_ref, down_ref, up_ref, bias_ref, proj_ref, pb_ref, *rest
):
    chunks, outs, scratch = rest[: -towers - 1], rest[-towers - 1 : -1], rest[-1]
    depth = chunks[0].shape[1]
    block = outs[0].shape[0]
    low = low_ref[...]
    for k, chunk in list(zip(ks, chunks, strict=True))[-late:]:
        at = pl.ds(pl.multiple_of((lax.axis_index("dev") ^ k) * depth, depth), depth)
        low += jnp.dot(chunk[...], down_ref[at, :], preferred_element_type=jnp.float32)
    low = low.astype(jnp.bfloat16)
    total = pb_ref[...]
    for k, chunk in zip(ks, chunks, strict=True):
        for first in range(0, depth, SPLIT):
            start = (lax.axis_index("dev") ^ k) * depth + first
            at = pl.ds(pl.multiple_of(start, SPLIT), SPLIT)
            high = jnp.dot(low, up_ref[:, at], preferred_element_type=jnp.float32)
            high = high + bias_ref[:, at]
            base = chunk[:, first : first + SPLIT].astype(jnp.float32)
            cross = (base * high + base).astype(jnp.bfloat16)
            total = total + jnp.dot(cross, proj_ref[at, :], preferred_element_type=jnp.float32)
    scratch[...] = total.astype(jnp.bfloat16)
    for k, out in enumerate(outs):
        out[...] = scratch[pl.ds(pl.multiple_of((lax.axis_index("tower") ^ k) * block, block), block), :]


def tower_out(low, down, up, bias, proj, pb, chunks, ks, late, towers):
    rows = chunks[0].shape[0]
    shape = jax.ShapeDtypeStruct((rows // towers, proj.shape[1]), jnp.bfloat16)
    return pl.pallas_call(
        functools.partial(tower_kernel, ks, late, towers),
        in_specs=[VMEM] * (6 + len(chunks)),
        out_specs=[VMEM] * towers,
        out_shape=[shape] + [pltpu.VMEM(shape.shape, shape.dtype)] * (towers - 1),
        scratch_shapes=[pltpu.VMEM((rows, proj.shape[1]), jnp.bfloat16)],
        compiler_params=pltpu.CompilerParams(vmem_limit_bytes=16 * MIB),
        cost_estimate=pl.CostEstimate(
            flops=4 * rows * proj.size, bytes_accessed=0, transcendentals=0
        ),
        name="tower_out",
    )(low, down, up, bias, proj, pb, *chunks)


def gram_kernel(*rest):
    chunks, out_ref, rows_ref = rest[:-2], rest[-2], rest[-1]
    towers, (block, width) = len(chunks), chunks[0].shape
    for i, chunk in enumerate(chunks):
        rows_ref[lax.axis_index("tower") ^ towers - 1 - i] = chunk[...]
    rows = rows_ref[...].reshape(towers * block, width)
    gram = lax.dot_general(
        rows, rows, (((1,), (1,)), ((), ())), preferred_element_type=jnp.float32
    ) * (1.0 / np.sqrt(np.float32(width)))
    n = towers * block
    at = lax.broadcasted_iota(jnp.int32, (block, n), 0)
    to = lax.broadcasted_iota(jnp.int32, (block, n), 1)
    own = at == lax.rem(to, block)
    place = 0
    for i in range(towers):
        picked = jnp.where(own, gram[i * block : (i + 1) * block], 0.0)
        line = jnp.sum(picked, axis=0, keepdims=True)
        for j in range(i + 1, towers):
            out_ref[place : place + 1, :] = line[:, j * block : (j + 1) * block]
            place += 1


def gram_pairs(chunks):
    towers, (block, width) = len(chunks), chunks[0].shape
    pairs = towers * (towers - 1) // 2
    return pl.pallas_call(
        gram_kernel,
        in_specs=[VMEM] * towers,
        out_specs=VMEM,
        out_shape=jax.ShapeDtypeStruct((pairs, block), jnp.float32),
        scratch_shapes=[pltpu.VMEM((towers, block, width), jnp.bfloat16)],
        compiler_params=pltpu.CompilerParams(vmem_limit_bytes=16 * MIB),
        name="gram_pairs",
    )(*chunks)


def swap(x, axis, k):
    size = lax.axis_size(axis)
    return lax.ppermute(x, axis, [(i, i ^ k) for i in range(size)])


def local(bag_ids, bag_lengths, tables, cross_down, cross_up, cross_bias, proj_weight, proj_bias):
    towers = lax.axis_size("tower")
    members = lax.axis_size("dev")
    samples = bag_ids.shape[1]
    block = samples // (towers * members)
    per = LANES // block
    groups = members // per
    ids = bag_ids[0].transpose(1, 2, 0)
    lens = bag_lengths[0].transpose(1, 0)
    bias = cross_bias[0]
    fixed = [ids, lens, tables[0], cross_down[0, 0], cross_up[0, 0], proj_weight[0]]
    ids, lens, rows, *weights = (pltpu.with_memory_space_constraint(w, pltpu.HBM) for w in fixed)
    down, up, proj = (pltpu.with_memory_space_constraint(w, pltpu.VMEM) for w in weights)
    far, near = list(range(per, members)), [1] + list(range(per - 1, 1, -1))
    order = far[:1] + near[:1] + far[1:2] + near[:0:-1] + far[:1:-1]
    batches = [far[:1], [0] + near[:1] + far[1:2], near[1:], far[2:]]
    steps = [far[:1], near[:1], far[1:2] + near[-1:] + [0] + near[1:-1]]
    pooled, got = {}, {}
    ids, lens, rows, *parts = pool_first(ids, lens, rows, batches[0], block, towers)
    pooled.update(zip(batches[0], parts, strict=True))
    for ks in batches[1:]:
        after = pltpu.with_memory_space_constraint(parts[0], pltpu.VMEM)
        parts = pool_more(ids, lens, rows, after, ks, block, towers)
        pooled.update(zip(ks, parts, strict=True))
    for k in order:
        got[k] = swap(pooled[k], "dev", k)
    got[0] = pooled[0]
    low = []
    for i, some in enumerate(steps):
        held = (up, proj) if i == 1 else ()
        low = [low_part(down, [got[k] for k in some], some, low, held)]
    done = [k for some in steps for k in some]
    ks = done + [k for k in [0] + order if k not in done]
    outs = tower_out(low[0], down, up, bias, proj, proj_bias, [got[k] for k in ks], ks, len(ks) - len(done), towers)
    met = [swap(outs[k], "tower", k) for k in range(towers - 1, 0, -1)] + [outs[0]]
    return gram_pairs(met).T


def solution(mesh):
    placed = (
        P("tower", None, "dev", None),
        P("tower", None, "dev"),
        P("tower", "dev", None, None),
        P("tower", None, None, None),
        P("tower", None, None, None),
        P("tower", None, None),
        P("tower", None, None),
        P("tower", None),
    )
    return jax.shard_map(
        local, mesh=mesh, in_specs=placed, out_specs=P(("tower", "dev"), None), check_vma=False
    )
```

```python
import functools

import jax
import jax.numpy as jnp
import numpy as np
from jax import lax
from jax.experimental import pallas as pl
from jax.experimental.pallas import tpu as pltpu
from jax.sharding import PartitionSpec as P

LANES = 128
MIB = 1 << 20
BATCH = 512
SPLIT = 256
ANY = pl.BlockSpec(memory_space=pl.ANY)
VMEM = pl.BlockSpec(memory_space=pltpu.VMEM)


def bag_columns(group, dest, block, towers, ids_ref, len_ref):
    feats, slots, samples = ids_ref.shape
    groups, per = samples // (towers * LANES), LANES // block
    lane = lax.broadcasted_iota(jnp.int32, (feats * slots, LANES), 1) // block
    columns = []
    for first in range(0, towers, per):
        bags = lens = None
        for q in range(per):
            start = ((first + q) * groups + group) * LANES
            at = pl.ds(pl.multiple_of(start, LANES), LANES)
            shift = lax.rem(q - dest + per, per) * block
            ids = jnp.concatenate([ids_ref[f, :, at] for f in range(feats)], axis=0)
            ids, own = pltpu.roll(ids, shift, 1), pltpu.roll(len_ref[:, at], shift, 1)
            bags = ids if bags is None else jnp.where(lane == q, ids, bags)
            lens = own if lens is None else jnp.where(lane[:feats] == q, own, lens)
        rows = []
        for f in range(feats):
            ids = bags[f * slots : (f + 1) * slots]
            slot = lax.broadcasted_iota(jnp.int32, ids.shape, 0)
            ids = jnp.where(slot < lens[f : f + 1], ids, -1)
            times = jnp.zeros(ids.shape, jnp.float32)
            for p in range(slots):
                times += jnp.where(ids == ids[p : p + 1], 1.0, 0.0)
            rows += [ids.astype(jnp.float32), times]
        rows = jnp.concatenate(rows, axis=0)
        columns.append(rows.T)
    return columns


def pool_rows(columns, f, slots, table):
    rows, table_rows = columns.shape[0], table.shape[0]
    place = lax.broadcasted_iota(jnp.int16, (rows, table_rows), 1)
    counts = jnp.zeros((rows, table_rows), jnp.bfloat16)
    for p in range(slots):
        c = 2 * slots * f + p
        own = columns[:, c : c + 1].astype(jnp.int32).astype(jnp.int16)
        times = columns[:, c + slots : c + slots + 1].astype(jnp.bfloat16)
        counts = jnp.where(place == own, times, counts)
    return jnp.dot(counts, table, preferred_element_type=jnp.float32).astype(jnp.bfloat16)


def pool_dests(group, dests, block, towers, ids_ref, len_ref, tables, outs, ready):
    (feats, slots, _), width = ids_ref.shape, tables.shape[2]
    height = outs[0].shape[0]
    batch = max(1, BATCH // height)
    for first in range(0, len(dests), batch):
        some = dests[first : first + batch]
        columns = [
            c for d in some for c in bag_columns(group, d, block, towers, ids_ref, len_ref)
        ]
        columns = jnp.concatenate(columns, axis=0) if len(columns) > 1 else columns[0]
        for f in range(feats):
            if ready is not None and first == 0:
                ready[f].wait()
            rows = pool_rows(columns, f, slots, tables[f])
            for i in range(len(some)):
                outs[first + i][:, f * width : (f + 1) * width] = rows[
                    i * height : (i + 1) * height
                ]


def pool_groups(ks, block, towers, ids_ref, len_ref, tab_ref, outs, ready=None):
    per = LANES // block
    me = lax.axis_index("dev")
    for g in sorted({k // per for k in ks}):
        some = [i for i, k in enumerate(ks) if k // per == g]
        dests = [lax.rem(me, per) ^ ks[i] % per for i in some]
        some = [outs[i] for i in some]
        pool_dests(me // per ^ g, dests, block, towers, ids_ref, len_ref, tab_ref, some, ready)
        ready = None


def first_kernel(ks, block, towers, ids_hbm, len_hbm, tab_hbm, ids_ref, len_ref, tab_ref, *rest):
    outs, sems = rest[:-1], rest[-1]
    feats = ids_ref.shape[0]
    bags = [
        pltpu.make_async_copy(ids_hbm, ids_ref, sems.at[0]),
        pltpu.make_async_copy(len_hbm, len_ref, sems.at[1]),
    ]
    rows = [
        pltpu.make_async_copy(tab_hbm.at[f], tab_ref.at[f], sems.at[2 + f]) for f in range(feats)
    ]
    for copy in bags + rows:
        copy.start()
    for copy in bags:
        copy.wait()
    pool_groups(ks, block, towers, ids_ref, len_ref, tab_ref, outs, rows)


def pool_first(ids, lens, tables, ks, block, towers):
    feats = ids.shape[0]
    shape = (towers * block, feats * tables.shape[2])
    return pl.pallas_call(
        functools.partial(first_kernel, ks, block, towers),
        in_specs=[ANY] * 3,
        out_specs=[VMEM] * (3 + len(ks)),
        out_shape=[jax.ShapeDtypeStruct(x.shape, x.dtype) for x in (ids, lens, tables)]
        + [pltpu.VMEM(shape, jnp.bfloat16)] * len(ks),
        scratch_shapes=[pltpu.SemaphoreType.DMA((2 + feats,))],
        compiler_params=pltpu.CompilerParams(vmem_limit_bytes=16 * MIB),
        name="pool_first",
    )(ids, lens, tables)


def more_kernel(ks, block, towers, ids_ref, len_ref, tab_ref, after_ref, *outs):
    pool_groups(ks, block, towers, ids_ref, len_ref, tab_ref, outs)


def pool_more(ids, lens, tables, after, ks, block, towers):
    shape = (towers * block, ids.shape[0] * tables.shape[2])
    return pl.pallas_call(
        functools.partial(more_kernel, ks, block, towers),
        in_specs=[VMEM, VMEM, VMEM, ANY],
        out_specs=[VMEM] * len(ks),
        out_shape=[pltpu.VMEM(shape, jnp.bfloat16)] * len(ks),
        compiler_params=pltpu.CompilerParams(vmem_limit_bytes=16 * MIB),
        cost_estimate=pl.CostEstimate(flops=2 * 10**9, bytes_accessed=0, transcendentals=0),
        name="pool_more",
    )(ids, lens, tables, after)


def low_kernel(ks, held, down_ref, *rest):
    chunks, low, out_ref = rest[: len(ks)], rest[len(ks) : -1 - held], rest[-1]
    depth = chunks[0].shape[1]
    total = low[0][...] if low else None
    for k, chunk in zip(ks, chunks, strict=True):
        at = pl.ds(pl.multiple_of((lax.axis_index("dev") ^ k) * depth, depth), depth)
        part = jnp.dot(chunk[...], down_ref[at, :], preferred_element_type=jnp.float32)
        total = part if total is None else total + part
    out_ref[...] = total


def low_part(down, chunks, ks, low, held=()):
    return pl.pallas_call(
        functools.partial(low_kernel, ks, len(held)),
        in_specs=[VMEM] * (1 + len(ks) + len(low)) + [ANY] * len(held),
        out_specs=VMEM,
        out_shape=jax.ShapeDtypeStruct((chunks[0].shape[0], down.shape[1]), jnp.float32),
        compiler_params=pltpu.CompilerParams(vmem_limit_bytes=16 * MIB),
        cost_estimate=pl.CostEstimate(flops=4 * 10**9, bytes_accessed=0, transcendentals=0),
        name="low_part",
    )(down, *chunks, *low, *held)


def tower_kernel(
    ks, late, towers, low_ref, down_ref, up_ref, bias_ref, proj_ref, pb_ref, *rest
):
    chunks, outs, scratch = rest[: -towers - 1], rest[-towers - 1 : -1], rest[-1]
    depth = chunks[0].shape[1]
    block = outs[0].shape[0]
    low = low_ref[...]
    for k, chunk in list(zip(ks, chunks, strict=True))[-late:]:
        at = pl.ds(pl.multiple_of((lax.axis_index("dev") ^ k) * depth, depth), depth)
        low += jnp.dot(chunk[...], down_ref[at, :], preferred_element_type=jnp.float32)
    low = low.astype(jnp.bfloat16)
    total = pb_ref[...]
    for k, chunk in zip(ks, chunks, strict=True):
        for first in range(0, depth, SPLIT):
            start = (lax.axis_index("dev") ^ k) * depth + first
            at = pl.ds(pl.multiple_of(start, SPLIT), SPLIT)
            high = jnp.dot(low, up_ref[:, at], preferred_element_type=jnp.float32)
            high = high + bias_ref[:, at]
            base = chunk[:, first : first + SPLIT].astype(jnp.float32)
            cross = (base * high + base).astype(jnp.bfloat16)
            total = total + jnp.dot(cross, proj_ref[at, :], preferred_element_type=jnp.float32)
    scratch[...] = total.astype(jnp.bfloat16)
    for k, out in enumerate(outs):
        out[...] = scratch[pl.ds(pl.multiple_of((lax.axis_index("tower") ^ k) * block, block), block), :]


def tower_out(low, down, up, bias, proj, pb, chunks, ks, late, towers):
    rows = chunks[0].shape[0]
    shape = jax.ShapeDtypeStruct((rows // towers, proj.shape[1]), jnp.bfloat16)
    return pl.pallas_call(
        functools.partial(tower_kernel, ks, late, towers),
        in_specs=[VMEM] * (6 + len(chunks)),
        out_specs=[VMEM] * towers,
        out_shape=[shape] + [pltpu.VMEM(shape.shape, shape.dtype)] * (towers - 1),
        scratch_shapes=[pltpu.VMEM((rows, proj.shape[1]), jnp.bfloat16)],
        compiler_params=pltpu.CompilerParams(vmem_limit_bytes=16 * MIB),
        cost_estimate=pl.CostEstimate(
            flops=4 * rows * proj.size, bytes_accessed=0, transcendentals=0
        ),
        name="tower_out",
    )(low, down, up, bias, proj, pb, *chunks)


def gram_kernel(*rest):
    chunks, out_ref, rows_ref = rest[:-2], rest[-2], rest[-1]
    towers, (block, width) = len(chunks), chunks[0].shape
    for i, chunk in enumerate(chunks):
        rows_ref[lax.axis_index("tower") ^ towers - 1 - i] = chunk[...]
    rows = rows_ref[...].reshape(towers * block, width)
    gram = lax.dot_general(
        rows, rows, (((1,), (1,)), ((), ())), preferred_element_type=jnp.float32
    ) * (1.0 / np.sqrt(np.float32(width)))
    n = towers * block
    at = lax.broadcasted_iota(jnp.int32, (block, n), 0)
    to = lax.broadcasted_iota(jnp.int32, (block, n), 1)
    own = at == lax.rem(to, block)
    place = 0
    for i in range(towers):
        picked = jnp.where(own, gram[i * block : (i + 1) * block], 0.0)
        line = jnp.sum(picked, axis=0, keepdims=True)
        for j in range(i + 1, towers):
            out_ref[place : place + 1, :] = line[:, j * block : (j + 1) * block]
            place += 1


def gram_pairs(chunks):
    towers, (block, width) = len(chunks), chunks[0].shape
    pairs = towers * (towers - 1) // 2
    return pl.pallas_call(
        gram_kernel,
        in_specs=[VMEM] * towers,
        out_specs=VMEM,
        out_shape=jax.ShapeDtypeStruct((pairs, block), jnp.float32),
        scratch_shapes=[pltpu.VMEM((towers, block, width), jnp.bfloat16)],
        compiler_params=pltpu.CompilerParams(vmem_limit_bytes=16 * MIB),
        name="gram_pairs",
    )(*chunks)


def swap(x, axis, k):
    size = lax.axis_size(axis)
    return lax.ppermute(x, axis, [(i, i ^ k) for i in range(size)])


def local(bag_ids, bag_lengths, tables, cross_down, cross_up, cross_bias, proj_weight, proj_bias):
    towers = lax.axis_size("tower")
    members = lax.axis_size("dev")
    samples = bag_ids.shape[1]
    block = samples // (towers * members)
    per = LANES // block
    groups = members // per
    ids = bag_ids[0].transpose(1, 2, 0)
    lens = bag_lengths[0].transpose(1, 0)
    bias = cross_bias[0]
    fixed = [ids, lens, tables[0], cross_down[0, 0], cross_up[0, 0], proj_weight[0]]
    ids, lens, rows, *weights = (pltpu.with_memory_space_constraint(w, pltpu.HBM) for w in fixed)
    down, up, proj = (pltpu.with_memory_space_constraint(w, pltpu.VMEM) for w in weights)
    far, near = list(range(per, members)), [1] + list(range(per - 1, 1, -1))
    order = far[:1] + near[:1] + far[1:2] + near[:0:-1] + far[:1:-1]
    batches = [far[:1], [0] + near[:1] + far[1:2], near[1:], far[2:]]
    steps = [far[:1], near[:1], far[1:2] + [0] + near[1:-1]]
    pooled, got = {}, {}
    ids, lens, rows, *parts = pool_first(ids, lens, rows, batches[0], block, towers)
    pooled.update(zip(batches[0], parts, strict=True))
    for ks in batches[1:]:
        after = pltpu.with_memory_space_constraint(parts[0], pltpu.VMEM)
        parts = pool_more(ids, lens, rows, after, ks, block, towers)
        pooled.update(zip(ks, parts, strict=True))
    for k in order:
        got[k] = swap(pooled[k], "dev", k)
    got[0] = pooled[0]
    low = []
    for i, some in enumerate(steps):
        held = (up, proj) if i == 1 else ()
        low = [low_part(down, [got[k] for k in some], some, low, held)]
    done = [k for some in steps for k in some]
    ks = done + [k for k in [0] + order if k not in done]
    outs = tower_out(low[0], down, up, bias, proj, proj_bias, [got[k] for k in ks], ks, len(ks) - len(done), towers)
    met = [swap(outs[k], "tower", k) for k in range(towers - 1, 0, -1)] + [outs[0]]
    return gram_pairs(met).T


def solution(mesh):
    placed = (
        P("tower", None, "dev", None),
        P("tower", None, "dev"),
        P("tower", "dev", None, None),
        P("tower", None, None, None),
        P("tower", None, None, None),
        P("tower", None, None),
        P("tower", None, None),
        P("tower", None),
    )
    return jax.shard_map(
        local, mesh=mesh, in_specs=placed, out_specs=P(("tower", "dev"), None), check_vma=False
    )
```

```python
import functools

import jax
import jax.numpy as jnp
import numpy as np
from jax import lax
from jax.experimental import pallas as pl
from jax.experimental.pallas import tpu as pltpu
from jax.sharding import PartitionSpec as P

LANES = 128
MIB = 1 << 20
BATCH = 512
SPLIT = 256
ANY = pl.BlockSpec(memory_space=pl.ANY)
VMEM = pl.BlockSpec(memory_space=pltpu.VMEM)


def bag_columns(group, dest, block, towers, ids_ref, len_ref):
    feats, slots, samples = ids_ref.shape
    groups, per = samples // (towers * LANES), LANES // block
    lane = lax.broadcasted_iota(jnp.int32, (feats * slots, LANES), 1) // block
    columns = []
    for first in range(0, towers, per):
        bags = lens = None
        for q in range(per):
            start = ((first + q) * groups + group) * LANES
            at = pl.ds(pl.multiple_of(start, LANES), LANES)
            shift = lax.rem(q - dest + per, per) * block
            ids = jnp.concatenate([ids_ref[f, :, at] for f in range(feats)], axis=0)
            ids, own = pltpu.roll(ids, shift, 1), pltpu.roll(len_ref[:, at], shift, 1)
            bags = ids if bags is None else jnp.where(lane == q, ids, bags)
            lens = own if lens is None else jnp.where(lane[:feats] == q, own, lens)
        rows = []
        for f in range(feats):
            ids = bags[f * slots : (f + 1) * slots]
            slot = lax.broadcasted_iota(jnp.int32, ids.shape, 0)
            ids = jnp.where(slot < lens[f : f + 1], ids, -1)
            times = jnp.zeros(ids.shape, jnp.float32)
            for p in range(slots):
                times += jnp.where(ids == ids[p : p + 1], 1.0, 0.0)
            rows += [ids.astype(jnp.float32), times]
        rows = jnp.concatenate(rows, axis=0)
        columns.append(rows.T)
    return columns


def pool_rows(columns, f, slots, table):
    rows, table_rows = columns.shape[0], table.shape[0]
    place = lax.broadcasted_iota(jnp.int16, (rows, table_rows), 1)
    counts = jnp.zeros((rows, table_rows), jnp.bfloat16)
    for p in range(slots):
        c = 2 * slots * f + p
        own = columns[:, c : c + 1].astype(jnp.int32).astype(jnp.int16)
        times = columns[:, c + slots : c + slots + 1].astype(jnp.bfloat16)
        counts = jnp.where(place == own, times, counts)
    return jnp.dot(counts, table, preferred_element_type=jnp.float32).astype(jnp.bfloat16)


def pool_dests(group, dests, block, towers, ids_ref, len_ref, tables, outs, ready):
    (feats, slots, _), width = ids_ref.shape, tables.shape[2]
    height = outs[0].shape[0]
    batch = max(1, BATCH // height)
    for first in range(0, len(dests), batch):
        some = dests[first : first + batch]
        columns = [
            c for d in some for c in bag_columns(group, d, block, towers, ids_ref, len_ref)
        ]
        columns = jnp.concatenate(columns, axis=0) if len(columns) > 1 else columns[0]
        for f in range(feats):
            if ready is not None and first == 0:
                ready[f].wait()
            rows = pool_rows(columns, f, slots, tables[f])
            for i in range(len(some)):
                outs[first + i][:, f * width : (f + 1) * width] = rows[
                    i * height : (i + 1) * height
                ]


def pool_groups(ks, block, towers, ids_ref, len_ref, tab_ref, outs, ready=None):
    per = LANES // block
    me = lax.axis_index("dev")
    for g in sorted({k // per for k in ks}):
        some = [i for i, k in enumerate(ks) if k // per == g]
        dests = [lax.rem(me, per) ^ ks[i] % per for i in some]
        some = [outs[i] for i in some]
        pool_dests(me // per ^ g, dests, block, towers, ids_ref, len_ref, tab_ref, some, ready)
        ready = None


def first_kernel(ks, block, towers, ids_hbm, len_hbm, tab_hbm, ids_ref, len_ref, tab_ref, *rest):
    outs, sems = rest[:-1], rest[-1]
    feats = ids_ref.shape[0]
    bags = [
        pltpu.make_async_copy(ids_hbm, ids_ref, sems.at[0]),
        pltpu.make_async_copy(len_hbm, len_ref, sems.at[1]),
    ]
    rows = [
        pltpu.make_async_copy(tab_hbm.at[f], tab_ref.at[f], sems.at[2 + f]) for f in range(feats)
    ]
    for copy in bags + rows:
        copy.start()
    for copy in bags:
        copy.wait()
    pool_groups(ks, block, towers, ids_ref, len_ref, tab_ref, outs, rows)


def pool_first(ids, lens, tables, ks, block, towers):
    feats = ids.shape[0]
    shape = (towers * block, feats * tables.shape[2])
    return pl.pallas_call(
        functools.partial(first_kernel, ks, block, towers),
        in_specs=[ANY] * 3,
        out_specs=[VMEM] * (3 + len(ks)),
        out_shape=[jax.ShapeDtypeStruct(x.shape, x.dtype) for x in (ids, lens, tables)]
        + [pltpu.VMEM(shape, jnp.bfloat16)] * len(ks),
        scratch_shapes=[pltpu.SemaphoreType.DMA((2 + feats,))],
        compiler_params=pltpu.CompilerParams(vmem_limit_bytes=16 * MIB),
        name="pool_first",
    )(ids, lens, tables)


def more_kernel(ks, block, towers, ids_ref, len_ref, tab_ref, after_ref, *outs):
    pool_groups(ks, block, towers, ids_ref, len_ref, tab_ref, outs)


def pool_more(ids, lens, tables, after, ks, block, towers):
    shape = (towers * block, ids.shape[0] * tables.shape[2])
    return pl.pallas_call(
        functools.partial(more_kernel, ks, block, towers),
        in_specs=[VMEM, VMEM, VMEM, ANY],
        out_specs=[VMEM] * len(ks),
        out_shape=[pltpu.VMEM(shape, jnp.bfloat16)] * len(ks),
        compiler_params=pltpu.CompilerParams(vmem_limit_bytes=16 * MIB),
        cost_estimate=pl.CostEstimate(flops=2 * 10**9, bytes_accessed=0, transcendentals=0),
        name="pool_more",
    )(ids, lens, tables, after)


def low_kernel(ks, held, down_ref, *rest):
    chunks, low, out_ref = rest[: len(ks)], rest[len(ks) : -1 - held], rest[-1]
    depth = chunks[0].shape[1]
    total = low[0][...] if low else None
    for k, chunk in zip(ks, chunks, strict=True):
        at = pl.ds(pl.multiple_of((lax.axis_index("dev") ^ k) * depth, depth), depth)
        part = jnp.dot(chunk[...], down_ref[at, :], preferred_element_type=jnp.float32)
        total = part if total is None else total + part
    out_ref[...] = total


def low_part(down, chunks, ks, low, held=()):
    return pl.pallas_call(
        functools.partial(low_kernel, ks, len(held)),
        in_specs=[VMEM] * (1 + len(ks) + len(low)) + [ANY] * len(held),
        out_specs=VMEM,
        out_shape=jax.ShapeDtypeStruct((chunks[0].shape[0], down.shape[1]), jnp.float32),
        compiler_params=pltpu.CompilerParams(vmem_limit_bytes=16 * MIB),
        cost_estimate=pl.CostEstimate(flops=4 * 10**9, bytes_accessed=0, transcendentals=0),
        name="low_part",
    )(down, *chunks, *low, *held)


def tower_kernel(
    ks, late, towers, low_ref, down_ref, up_ref, bias_ref, proj_ref, pb_ref, *rest
):
    chunks, outs, scratch = rest[: -towers - 1], rest[-towers - 1 : -1], rest[-1]
    depth = chunks[0].shape[1]
    block = outs[0].shape[0]
    low = low_ref[...]
    for k, chunk in list(zip(ks, chunks, strict=True))[-late:]:
        at = pl.ds(pl.multiple_of((lax.axis_index("dev") ^ k) * depth, depth), depth)
        low += jnp.dot(chunk[...], down_ref[at, :], preferred_element_type=jnp.float32)
    low = low.astype(jnp.bfloat16)
    total = pb_ref[...]
    for k, chunk in zip(ks, chunks, strict=True):
        for first in range(0, depth, SPLIT):
            start = (lax.axis_index("dev") ^ k) * depth + first
            at = pl.ds(pl.multiple_of(start, SPLIT), SPLIT)
            high = jnp.dot(low, up_ref[:, at], preferred_element_type=jnp.float32)
            high = high + bias_ref[:, at]
            base = chunk[:, first : first + SPLIT].astype(jnp.float32)
            cross = (base * high + base).astype(jnp.bfloat16)
            total = total + jnp.dot(cross, proj_ref[at, :], preferred_element_type=jnp.float32)
    scratch[...] = total.astype(jnp.bfloat16)
    for k, out in enumerate(outs):
        out[...] = scratch[pl.ds(pl.multiple_of((lax.axis_index("tower") ^ k) * block, block), block), :]


def tower_out(low, down, up, bias, proj, pb, chunks, ks, late, towers):
    rows = chunks[0].shape[0]
    shape = jax.ShapeDtypeStruct((rows // towers, proj.shape[1]), jnp.bfloat16)
    return pl.pallas_call(
        functools.partial(tower_kernel, ks, late, towers),
        in_specs=[VMEM] * (6 + len(chunks)),
        out_specs=[VMEM] * towers,
        out_shape=[shape] + [pltpu.VMEM(shape.shape, shape.dtype)] * (towers - 1),
        scratch_shapes=[pltpu.VMEM((rows, proj.shape[1]), jnp.bfloat16)],
        compiler_params=pltpu.CompilerParams(vmem_limit_bytes=16 * MIB),
        cost_estimate=pl.CostEstimate(
            flops=4 * rows * proj.size, bytes_accessed=0, transcendentals=0
        ),
        name="tower_out",
    )(low, down, up, bias, proj, pb, *chunks)


def gram_kernel(*rest):
    chunks, out_ref, rows_ref = rest[:-2], rest[-2], rest[-1]
    towers, (block, width) = len(chunks), chunks[0].shape
    for i, chunk in enumerate(chunks):
        rows_ref[lax.axis_index("tower") ^ towers - 1 - i] = chunk[...]
    rows = rows_ref[...].reshape(towers * block, width)
    gram = lax.dot_general(
        rows, rows, (((1,), (1,)), ((), ())), preferred_element_type=jnp.float32
    ) * (1.0 / np.sqrt(np.float32(width)))
    n = towers * block
    at = lax.broadcasted_iota(jnp.int32, (block, n), 0)
    to = lax.broadcasted_iota(jnp.int32, (block, n), 1)
    own = at == lax.rem(to, block)
    place = 0
    for i in range(towers):
        picked = jnp.where(own, gram[i * block : (i + 1) * block], 0.0)
        line = jnp.sum(picked, axis=0, keepdims=True)
        for j in range(i + 1, towers):
            out_ref[place : place + 1, :] = line[:, j * block : (j + 1) * block]
            place += 1


def gram_pairs(chunks):
    towers, (block, width) = len(chunks), chunks[0].shape
    pairs = towers * (towers - 1) // 2
    return pl.pallas_call(
        gram_kernel,
        in_specs=[VMEM] * towers,
        out_specs=VMEM,
        out_shape=jax.ShapeDtypeStruct((pairs, block), jnp.float32),
        scratch_shapes=[pltpu.VMEM((towers, block, width), jnp.bfloat16)],
        compiler_params=pltpu.CompilerParams(vmem_limit_bytes=16 * MIB),
        name="gram_pairs",
    )(*chunks)


def swap(x, axis, k):
    size = lax.axis_size(axis)
    return lax.ppermute(x, axis, [(i, i ^ k) for i in range(size)])


def local(bag_ids, bag_lengths, tables, cross_down, cross_up, cross_bias, proj_weight, proj_bias):
    towers = lax.axis_size("tower")
    members = lax.axis_size("dev")
    samples = bag_ids.shape[1]
    block = samples // (towers * members)
    per = LANES // block
    groups = members // per
    ids = bag_ids[0].transpose(1, 2, 0)
    lens = bag_lengths[0].transpose(1, 0)
    bias = cross_bias[0]
    fixed = [ids, lens, tables[0], cross_down[0, 0], cross_up[0, 0], proj_weight[0]]
    ids, lens, rows, *weights = (pltpu.with_memory_space_constraint(w, pltpu.HBM) for w in fixed)
    down, up, proj = (pltpu.with_memory_space_constraint(w, pltpu.VMEM) for w in weights)
    far, near = list(range(per, members)), [1] + list(range(per - 1, 1, -1))
    order = far[:1] + near[:1] + far[1:2] + near[:0:-1] + far[:1:-1]
    batches = [far[:1], [0] + near[:1] + far[1:2], near[1:], far[2:]]
    steps = [far[:1], near[:1], [0] + near[1:-1], far[1:2]]
    pooled, got = {}, {}
    ids, lens, rows, *parts = pool_first(ids, lens, rows, batches[0], block, towers)
    pooled.update(zip(batches[0], parts, strict=True))
    for ks in batches[1:]:
        after = pltpu.with_memory_space_constraint(parts[0], pltpu.VMEM)
        parts = pool_more(ids, lens, rows, after, ks, block, towers)
        pooled.update(zip(ks, parts, strict=True))
    for k in order:
        got[k] = swap(pooled[k], "dev", k)
    got[0] = pooled[0]
    low = []
    for i, some in enumerate(steps):
        held = (up, proj) if i == 1 else ()
        low = [low_part(down, [got[k] for k in some], some, low, held)]
    done = [k for some in steps for k in some]
    ks = done + [k for k in [0] + order if k not in done]
    outs = tower_out(low[0], down, up, bias, proj, proj_bias, [got[k] for k in ks], ks, len(ks) - len(done), towers)
    met = [swap(outs[k], "tower", k) for k in range(towers - 1, 0, -1)] + [outs[0]]
    return gram_pairs(met).T


def solution(mesh):
    placed = (
        P("tower", None, "dev", None),
        P("tower", None, "dev"),
        P("tower", "dev", None, None),
        P("tower", None, None, None),
        P("tower", None, None, None),
        P("tower", None, None),
        P("tower", None, None),
        P("tower", None),
    )
    return jax.shard_map(
        local, mesh=mesh, in_specs=placed, out_specs=P(("tower", "dev"), None), check_vma=False
    )
```

```python
import functools

import jax
import jax.numpy as jnp
import numpy as np
from jax import lax
from jax.experimental import pallas as pl
from jax.experimental.pallas import tpu as pltpu
from jax.sharding import PartitionSpec as P

LANES = 128
MIB = 1 << 20
BATCH = 512
SPLIT = 256
ANY = pl.BlockSpec(memory_space=pl.ANY)
VMEM = pl.BlockSpec(memory_space=pltpu.VMEM)


def bag_columns(group, dest, block, towers, ids_ref, len_ref):
    feats, slots, samples = ids_ref.shape
    groups, per = samples // (towers * LANES), LANES // block
    lane = lax.broadcasted_iota(jnp.int32, (feats * slots, LANES), 1) // block
    columns = []
    for first in range(0, towers, per):
        bags = lens = None
        for q in range(per):
            start = ((first + q) * groups + group) * LANES
            at = pl.ds(pl.multiple_of(start, LANES), LANES)
            shift = lax.rem(q - dest + per, per) * block
            ids = jnp.concatenate([ids_ref[f, :, at] for f in range(feats)], axis=0)
            ids, own = pltpu.roll(ids, shift, 1), pltpu.roll(len_ref[:, at], shift, 1)
            bags = ids if bags is None else jnp.where(lane == q, ids, bags)
            lens = own if lens is None else jnp.where(lane[:feats] == q, own, lens)
        rows = []
        for f in range(feats):
            ids = bags[f * slots : (f + 1) * slots]
            slot = lax.broadcasted_iota(jnp.int32, ids.shape, 0)
            ids = jnp.where(slot < lens[f : f + 1], ids, -1)
            times = jnp.zeros(ids.shape, jnp.float32)
            for p in range(slots):
                times += jnp.where(ids == ids[p : p + 1], 1.0, 0.0)
            rows += [ids.astype(jnp.float32), times]
        rows = jnp.concatenate(rows, axis=0)
        columns.append(rows.T)
    return columns


def pool_rows(columns, f, slots, table):
    blocks = []
    for first in range(0, columns.shape[0], LANES):
        own = columns[first : first + LANES, 2 * slots * f : 2 * slots * (f + 1)]
        ids = own[:, :slots].astype(jnp.int32).astype(jnp.int16)
        times = own[:, slots:].astype(jnp.bfloat16)
        total = None
        for start in range(0, table.shape[0], SPLIT):
            place = lax.broadcasted_iota(jnp.int16, (LANES, SPLIT), 1) + jnp.int16(start)
            counts = jnp.zeros((LANES, SPLIT), jnp.bfloat16)
            for p in range(slots):
                counts = jnp.where(place == ids[:, p : p + 1], times[:, p : p + 1], counts)
            part = jnp.dot(
                counts, table[start : start + SPLIT], preferred_element_type=jnp.float32
            )
            total = part if total is None else total + part
        blocks.append(total.astype(jnp.bfloat16))
    return jnp.concatenate(blocks, axis=0) if len(blocks) > 1 else blocks[0]


def pool_dests(group, dests, block, towers, ids_ref, len_ref, tables, outs, ready):
    (feats, slots, _), width = ids_ref.shape, tables.shape[2]
    height = outs[0].shape[0]
    batch = max(1, BATCH // height)
    for first in range(0, len(dests), batch):
        some = dests[first : first + batch]
        columns = [
            c for d in some for c in bag_columns(group, d, block, towers, ids_ref, len_ref)
        ]
        columns = jnp.concatenate(columns, axis=0) if len(columns) > 1 else columns[0]
        for f in range(feats):
            if ready is not None and first == 0:
                ready[f].wait()
            rows = pool_rows(columns, f, slots, tables[f])
            for i in range(len(some)):
                outs[first + i][:, f * width : (f + 1) * width] = rows[
                    i * height : (i + 1) * height
                ]


def pool_groups(ks, block, towers, ids_ref, len_ref, tab_ref, outs, ready=None):
    per = LANES // block
    me = lax.axis_index("dev")
    for g in sorted({k // per for k in ks}):
        some = [i for i, k in enumerate(ks) if k // per == g]
        dests = [lax.rem(me, per) ^ ks[i] % per for i in some]
        some = [outs[i] for i in some]
        pool_dests(me // per ^ g, dests, block, towers, ids_ref, len_ref, tab_ref, some, ready)
        ready = None


def first_kernel(ks, block, towers, ids_hbm, len_hbm, tab_hbm, ids_ref, len_ref, tab_ref, *rest):
    outs, sems = rest[:-1], rest[-1]
    feats = ids_ref.shape[0]
    bags = [
        pltpu.make_async_copy(ids_hbm, ids_ref, sems.at[0]),
        pltpu.make_async_copy(len_hbm, len_ref, sems.at[1]),
    ]
    rows = [
        pltpu.make_async_copy(tab_hbm.at[f], tab_ref.at[f], sems.at[2 + f]) for f in range(feats)
    ]
    for copy in bags + rows:
        copy.start()
    for copy in bags:
        copy.wait()
    pool_groups(ks, block, towers, ids_ref, len_ref, tab_ref, outs, rows)


def pool_first(ids, lens, tables, ks, block, towers):
    feats = ids.shape[0]
    shape = (towers * block, feats * tables.shape[2])
    return pl.pallas_call(
        functools.partial(first_kernel, ks, block, towers),
        in_specs=[ANY] * 3,
        out_specs=[VMEM] * (3 + len(ks)),
        out_shape=[jax.ShapeDtypeStruct(x.shape, x.dtype) for x in (ids, lens, tables)]
        + [pltpu.VMEM(shape, jnp.bfloat16)] * len(ks),
        scratch_shapes=[pltpu.SemaphoreType.DMA((2 + feats,))],
        compiler_params=pltpu.CompilerParams(vmem_limit_bytes=16 * MIB),
        name="pool_first",
    )(ids, lens, tables)


def more_kernel(ks, block, towers, ids_ref, len_ref, tab_ref, after_ref, *outs):
    pool_groups(ks, block, towers, ids_ref, len_ref, tab_ref, outs)


def pool_more(ids, lens, tables, after, ks, block, towers):
    shape = (towers * block, ids.shape[0] * tables.shape[2])
    return pl.pallas_call(
        functools.partial(more_kernel, ks, block, towers),
        in_specs=[VMEM, VMEM, VMEM, ANY],
        out_specs=[VMEM] * len(ks),
        out_shape=[pltpu.VMEM(shape, jnp.bfloat16)] * len(ks),
        compiler_params=pltpu.CompilerParams(vmem_limit_bytes=16 * MIB),
        cost_estimate=pl.CostEstimate(flops=2 * 10**9, bytes_accessed=0, transcendentals=0),
        name="pool_more",
    )(ids, lens, tables, after)


def low_kernel(ks, held, down_ref, *rest):
    chunks, low, out_ref = rest[: len(ks)], rest[len(ks) : -1 - held], rest[-1]
    depth = chunks[0].shape[1]
    total = low[0][...] if low else None
    for k, chunk in zip(ks, chunks, strict=True):
        at = pl.ds(pl.multiple_of((lax.axis_index("dev") ^ k) * depth, depth), depth)
        part = jnp.dot(chunk[...], down_ref[at, :], preferred_element_type=jnp.float32)
        total = part if total is None else total + part
    out_ref[...] = total


def low_part(down, chunks, ks, low, held=()):
    return pl.pallas_call(
        functools.partial(low_kernel, ks, len(held)),
        in_specs=[VMEM] * (1 + len(ks) + len(low)) + [ANY] * len(held),
        out_specs=VMEM,
        out_shape=jax.ShapeDtypeStruct((chunks[0].shape[0], down.shape[1]), jnp.float32),
        compiler_params=pltpu.CompilerParams(vmem_limit_bytes=16 * MIB),
        cost_estimate=pl.CostEstimate(flops=4 * 10**9, bytes_accessed=0, transcendentals=0),
        name="low_part",
    )(down, *chunks, *low, *held)


def tower_kernel(
    ks, late, towers, low_ref, down_ref, up_ref, bias_ref, proj_ref, pb_ref, *rest
):
    chunks, outs, scratch = rest[: -towers - 1], rest[-towers - 1 : -1], rest[-1]
    depth = chunks[0].shape[1]
    block = outs[0].shape[0]
    low = low_ref[...]
    for k, chunk in list(zip(ks, chunks, strict=True))[-late:]:
        at = pl.ds(pl.multiple_of((lax.axis_index("dev") ^ k) * depth, depth), depth)
        low += jnp.dot(chunk[...], down_ref[at, :], preferred_element_type=jnp.float32)
    low = low.astype(jnp.bfloat16)
    total = pb_ref[...]
    for k, chunk in zip(ks, chunks, strict=True):
        for first in range(0, depth, SPLIT):
            start = (lax.axis_index("dev") ^ k) * depth + first
            at = pl.ds(pl.multiple_of(start, SPLIT), SPLIT)
            high = jnp.dot(low, up_ref[:, at], preferred_element_type=jnp.float32)
            high = high + bias_ref[:, at]
            base = chunk[:, first : first + SPLIT].astype(jnp.float32)
            cross = (base * high + base).astype(jnp.bfloat16)
            total = total + jnp.dot(cross, proj_ref[at, :], preferred_element_type=jnp.float32)
    scratch[...] = total.astype(jnp.bfloat16)
    for k, out in enumerate(outs):
        out[...] = scratch[pl.ds(pl.multiple_of((lax.axis_index("tower") ^ k) * block, block), block), :]


def tower_out(low, down, up, bias, proj, pb, chunks, ks, late, towers):
    rows = chunks[0].shape[0]
    shape = jax.ShapeDtypeStruct((rows // towers, proj.shape[1]), jnp.bfloat16)
    return pl.pallas_call(
        functools.partial(tower_kernel, ks, late, towers),
        in_specs=[VMEM] * (6 + len(chunks)),
        out_specs=[VMEM] * towers,
        out_shape=[shape] + [pltpu.VMEM(shape.shape, shape.dtype)] * (towers - 1),
        scratch_shapes=[pltpu.VMEM((rows, proj.shape[1]), jnp.bfloat16)],
        compiler_params=pltpu.CompilerParams(vmem_limit_bytes=16 * MIB),
        cost_estimate=pl.CostEstimate(
            flops=4 * rows * proj.size, bytes_accessed=0, transcendentals=0
        ),
        name="tower_out",
    )(low, down, up, bias, proj, pb, *chunks)


def gram_kernel(*rest):
    chunks, out_ref, rows_ref = rest[:-2], rest[-2], rest[-1]
    towers, (block, width) = len(chunks), chunks[0].shape
    for i, chunk in enumerate(chunks):
        rows_ref[lax.axis_index("tower") ^ towers - 1 - i] = chunk[...]
    rows = rows_ref[...].reshape(towers * block, width)
    gram = lax.dot_general(
        rows, rows, (((1,), (1,)), ((), ())), preferred_element_type=jnp.float32
    ) * (1.0 / np.sqrt(np.float32(width)))
    n = towers * block
    at = lax.broadcasted_iota(jnp.int32, (block, n), 0)
    to = lax.broadcasted_iota(jnp.int32, (block, n), 1)
    own = at == lax.rem(to, block)
    place = 0
    for i in range(towers):
        picked = jnp.where(own, gram[i * block : (i + 1) * block], 0.0)
        line = jnp.sum(picked, axis=0, keepdims=True)
        for j in range(i + 1, towers):
            out_ref[place : place + 1, :] = line[:, j * block : (j + 1) * block]
            place += 1


def gram_pairs(chunks):
    towers, (block, width) = len(chunks), chunks[0].shape
    pairs = towers * (towers - 1) // 2
    return pl.pallas_call(
        gram_kernel,
        in_specs=[VMEM] * towers,
        out_specs=VMEM,
        out_shape=jax.ShapeDtypeStruct((pairs, block), jnp.float32),
        scratch_shapes=[pltpu.VMEM((towers, block, width), jnp.bfloat16)],
        compiler_params=pltpu.CompilerParams(vmem_limit_bytes=16 * MIB),
        name="gram_pairs",
    )(*chunks)


def swap(x, axis, k):
    size = lax.axis_size(axis)
    return lax.ppermute(x, axis, [(i, i ^ k) for i in range(size)])


def local(bag_ids, bag_lengths, tables, cross_down, cross_up, cross_bias, proj_weight, proj_bias):
    towers = lax.axis_size("tower")
    members = lax.axis_size("dev")
    samples = bag_ids.shape[1]
    block = samples // (towers * members)
    per = LANES // block
    groups = members // per
    ids = bag_ids[0].transpose(1, 2, 0)
    lens = bag_lengths[0].transpose(1, 0)
    bias = cross_bias[0]
    fixed = [ids, lens, tables[0], cross_down[0, 0], cross_up[0, 0], proj_weight[0]]
    ids, lens, rows, *weights = (pltpu.with_memory_space_constraint(w, pltpu.HBM) for w in fixed)
    down, up, proj = (pltpu.with_memory_space_constraint(w, pltpu.VMEM) for w in weights)
    far, near = list(range(per, members)), [1] + list(range(per - 1, 1, -1))
    order = far[:1] + near[:1] + far[1:2] + near[:0:-1] + far[:1:-1]
    batches = [far[:1], [0] + near[:1] + far[1:2], near[1:], far[2:]]
    steps = [far[:1], near[:1], far[1:2] + [0] + near[1:-1]]
    pooled, got = {}, {}
    ids, lens, rows, *parts = pool_first(ids, lens, rows, batches[0], block, towers)
    pooled.update(zip(batches[0], parts, strict=True))
    for ks in batches[1:]:
        after = pltpu.with_memory_space_constraint(parts[0], pltpu.VMEM)
        parts = pool_more(ids, lens, rows, after, ks, block, towers)
        pooled.update(zip(ks, parts, strict=True))
    for k in order:
        got[k] = swap(pooled[k], "dev", k)
    got[0] = pooled[0]
    low = []
    for i, some in enumerate(steps):
        held = (up, proj) if i == 1 else ()
        low = [low_part(down, [got[k] for k in some], some, low, held)]
    done = [k for some in steps for k in some]
    ks = done + [k for k in [0] + order if k not in done]
    outs = tower_out(low[0], down, up, bias, proj, proj_bias, [got[k] for k in ks], ks, len(ks) - len(done), towers)
    met = [swap(outs[k], "tower", k) for k in range(towers - 1, 0, -1)] + [outs[0]]
    return gram_pairs(met).T


def solution(mesh):
    placed = (
        P("tower", None, "dev", None),
        P("tower", None, "dev"),
        P("tower", "dev", None, None),
        P("tower", None, None, None),
        P("tower", None, None, None),
        P("tower", None, None),
        P("tower", None, None),
        P("tower", None),
    )
    return jax.shard_map(
        local, mesh=mesh, in_specs=placed, out_specs=P(("tower", "dev"), None), check_vma=False
    )
```
